256 devices in a mesh: tm: 8 (over y, core), height: 8 (over x, z_hi), heads: 4 (over z_lo).
Axes of the slice: x: 4, y: 4, z: 8 (z_hi: 2, z_lo: 4; z = z_hi * 4 + z_lo), core: 2. Of those that a mesh axis runs over, the one named last changes fastest.
Arguments:
- q_raw: bfloat16 [48, 64, 4, 1536], P('tm', 'height', None, 'heads'), may hold values from -4 to 4
- k_raw: bfloat16 [48, 64, 4, 1536], P('tm', 'height', None, 'heads'), may hold values from -4 to 4
- value_in: bfloat16 [48, 64, 4, 1536], P('tm', 'height', None, 'heads'), may hold values from -6 to 6
- out_grad: bfloat16 [48, 64, 4, 1536], P('tm', 'height', None, 'heads'), may hold values from -6 to 6
- q_gain: float32 [128], replicated, may hold values from 0.3 to 5
- k_gain: float32 [128], replicated, may hold values from 0.3 to 5
Outputs:
- q_grad: bfloat16 [48, 64, 4, 1536], P('tm', 'height', None, 'heads')
- k_grad: bfloat16 [48, 64, 4, 1536], P('tm', 'height', None, 'heads')
- v_grad: bfloat16 [48, 64, 4, 1536], P('tm', 'height', None, 'heads')
- q_gain_grad: float32 [128], replicated
- k_gain_grad: float32 [128], replicated
The draws below stay inside these ranges and needn't reach their ends.
All inputs are finite; a program needn't handle non-finite values.
Results may differ from the reference program's by a relative error of at most 0.038.
The reference program's roundings to bfloat16 on the way count: a program that leaves them out, or rounds other values in their place, can miss the bound.
Values may be sent and summed in bfloat16 or wider, within the bound.
No kernel may reach another device: no remote copies, remote signals or barrier semaphores. Data moves between devices by JAX's collectives and lax.ppermute only.
A program may use at most 64 MiB of HBM per device.

```python
import math
import jax
import jax.numpy as jnp
from jax import lax

TILE_T = 6
TILE_H = 8
TILE_W = 4
WIDTH_TILES = 1
HEAD_DIM = 128
TILE = 192
FRAMES = 48
ROWS = 64
COLS = 4
HEADS = 12
N_TM = 8
N_HEIGHT = 8


def draw_k_raw(key, part):
    key = jax.random.fold_in(key, 11)
    noise = jnp.clip(jax.random.normal(key, (FRAMES, ROWS, COLS, HEADS, HEAD_DIM), jnp.float32), -4.0, 4.0)
    return noise.reshape(FRAMES, ROWS, COLS, HEADS * HEAD_DIM).astype(jnp.bfloat16)


def draw_q_raw(key, part):
    key = jax.random.fold_in(key, 12)
    noise = jnp.clip(jax.random.normal(key, (FRAMES, ROWS, COLS, HEADS, HEAD_DIM), jnp.float32), -4.0, 4.0)
    return noise.reshape(FRAMES, ROWS, COLS, HEADS * HEAD_DIM).astype(jnp.bfloat16)


def gain_values(key):
    return jnp.exp(jax.random.uniform(key, (HEAD_DIM,), jnp.float32, math.log(0.5), math.log(2.0)))


def draw_q_gain(key, part):
    key = jax.random.fold_in(key, 21)
    return gain_values(key)


def draw_k_gain(key, part):
    key = jax.random.fold_in(key, 22)
    return gain_values(key)


def block_scale(rng, shape, cuts, low, top_value):
    loudness = 1.0
    for dim, shards_of in cuts:
        steps = jax.random.uniform(jax.random.fold_in(jax.random.fold_in(rng, 6), dim), (shards_of,), jnp.float32, low / len(cuts), top_value / len(cuts))
        loudness = loudness * jnp.repeat(jnp.exp(steps), shape[dim] // shards_of).reshape((-1,) + (1,) * (len(shape) - 1 - dim))
    return loudness


def centred(rng, extent, deviation, reach, pieces=(), held_as=jnp.bfloat16):
    factor_of = block_scale(rng, extent, pieces, -0.22, 0.18) if pieces else 1.0
    entries = jax.random.normal(rng, extent, jnp.float32) * deviation * factor_of
    return jnp.minimum(jnp.maximum(entries, -reach), reach).astype(held_as)


def setup_inputs(seed: int = 0) -> dict:
    splits = jax.random.split(jax.random.key(seed), 7)
    return {
        "q_raw": draw_q_raw(jax.random.fold_in(splits[6], 71), 0),
        "k_raw": draw_k_raw(jax.random.fold_in(splits[6], 71), 0),
        "value_in": centred(splits[2], (FRAMES, ROWS, COLS, HEADS * HEAD_DIM), 1.0, 6.0, ((0, 8), (1, 8), (3, 4))),
        "out_grad": centred(splits[3], (FRAMES, ROWS, COLS, HEADS * HEAD_DIM), 1.0, 6.0, ((0, 8), (1, 8), (3, 4))),
        "q_gain": draw_q_gain(jax.random.fold_in(splits[6], 71), 0),
        "k_gain": draw_k_gain(jax.random.fold_in(splits[6], 71), 0),
    }


eps = 1e-06

def to_tiles(array):
    grid = array.reshape(N_TM, TILE_T, N_HEIGHT, TILE_H, WIDTH_TILES, TILE_W, HEADS, HEAD_DIM)
    grid = grid.transpose(0, 2, 4, 1, 3, 5, 6, 7)
    return grid.reshape(N_TM, N_HEIGHT, WIDTH_TILES, TILE, HEADS, HEAD_DIM)

def from_tiles(array):
    grid = array.reshape(N_TM, N_HEIGHT, WIDTH_TILES, TILE_T, TILE_H, TILE_W, HEADS * HEAD_DIM)
    grid = grid.transpose(0, 3, 1, 4, 2, 5, 6)
    return grid.reshape(FRAMES, ROWS, COLS, HEADS * HEAD_DIM)

def rounded(array):
    return lax.optimization_barrier(array.astype(jnp.bfloat16)).astype(jnp.float32)

def normalize(raw, gain):
    values = raw.astype(jnp.float32)
    inverse = lax.rsqrt(lax.optimization_barrier(jnp.mean(values * values, axis=-1, keepdims=True)) + eps)
    unit = values * inverse
    return (unit, inverse, rounded(unit * gain))

def norm_back(grad_norm, unit, inverse, gain):
    grad_unit = grad_norm * gain
    inner = lax.optimization_barrier(jnp.mean(grad_unit * unit, axis=-1, keepdims=True))
    raw_grad = ((grad_unit - unit * inner) * inverse).astype(jnp.bfloat16)
    gain_terms = lax.optimization_barrier(jnp.sum((grad_norm * unit).reshape(-1, unit.shape[-1]), axis=0))
    return (raw_grad, gain_terms)

def query_side(queries, grad_rows, span_keys, span_values, allowed, score_scale):
    scores = jnp.einsum('qhd,khd->hqk', queries, span_keys) * score_scale
    scores = jnp.where(allowed[None, None, :], scores, -jnp.inf)
    highest = lax.optimization_barrier(jnp.max(scores, axis=-1, keepdims=True))
    summed = lax.optimization_barrier(jnp.sum(jnp.exp(scores - highest), axis=-1, keepdims=True))
    log_total = highest + jnp.log(summed)
    probability = jnp.exp(scores - log_total)
    weights = rounded(probability)
    output = rounded(jnp.einsum('hqk,khd->qhd', weights, span_values))
    delta = lax.optimization_barrier(jnp.sum(grad_rows * output, axis=-1)).T
    prob_grad = jnp.einsum('qhd,khd->hqk', grad_rows, span_values)
    score_grad = rounded(probability * (prob_grad - delta[:, :, None]))
    query_grad = jnp.einsum('hqk,khd->qhd', score_grad, span_keys) * score_scale
    return (log_total[:, :, 0], delta, query_grad)

def key_side(own_keys, own_values, span_queries, span_grads, span_totals, span_deltas, allowed, score_scale):
    scores = jnp.einsum('qhd,khd->hqk', span_queries, own_keys) * score_scale
    scores = jnp.where(allowed[None, :, None], scores, -jnp.inf)
    probability = jnp.exp(scores - span_totals[:, :, None])
    weights = rounded(probability)
    value_grad = jnp.einsum('hqk,qhd->khd', weights, span_grads)
    prob_grad = jnp.einsum('qhd,khd->hqk', span_grads, own_values)
    score_grad = rounded(probability * (prob_grad - span_deltas[:, :, None]))
    key_grad = jnp.einsum('hqk,qhd->khd', score_grad, span_queries) * score_scale
    return (key_grad, value_grad)

def reference(q_raw, k_raw, value_in, out_grad, q_gain, k_gain):
    score_scale = 1.0 / math.sqrt(HEAD_DIM)
    q_unit, q_inverse, q_norm = normalize(to_tiles(q_raw), q_gain)
    k_unit, k_inverse, k_norm = normalize(to_tiles(k_raw), k_gain)
    values = to_tiles(value_in).astype(jnp.float32)
    grad_rows = to_tiles(out_grad).astype(jnp.float32)
    margin = ((1, 1), (1, 1), (0, 0), (0, 0), (0, 0), (0, 0))
    keys_wide = jnp.pad(k_norm, margin)
    values_wide = jnp.pad(values, margin)
    queries_wide = jnp.pad(q_norm, margin)
    grads_wide = jnp.pad(grad_rows, margin)
    present = jnp.pad(jnp.ones((N_TM, N_HEIGHT), jnp.int32), 1)

    def window(padded, frame_tile, row_tile):
        zero = frame_tile * 0
        starts = (frame_tile, row_tile) + (zero,) * (padded.ndim - 2)
        return lax.dynamic_slice(padded, starts, (3, 3) + padded.shape[2:])

    def allowed_mask(frame_tile, row_tile, span_len):
        near = lax.dynamic_slice(present, (frame_tile, row_tile), (3, 3))
        return jnp.broadcast_to(near[:, :, None, None] > 0, (3, 3, span_len, TILE)).reshape(-1)

    def first_pass(position):
        frame_tile = position // N_HEIGHT
        row_tile = position % N_HEIGHT
        near_keys = window(keys_wide, frame_tile, row_tile)
        near_values = window(values_wide, frame_tile, row_tile)
        own_queries = q_norm[frame_tile, row_tile]
        own_grads = grad_rows[frame_tile, row_tile]
        results = []
        for width_tile in range(WIDTH_TILES):
            start_w = max(0, width_tile - 1)
            stop_w = min(WIDTH_TILES, width_tile + 2)
            span_keys = near_keys[:, :, start_w:stop_w].reshape(-1, HEADS, HEAD_DIM)
            span_values = near_values[:, :, start_w:stop_w].reshape(-1, HEADS, HEAD_DIM)
            allowed = allowed_mask(frame_tile, row_tile, stop_w - start_w)
            results.append(query_side(own_queries[width_tile], own_grads[width_tile], span_keys, span_values, allowed, score_scale))
        return tuple((jnp.stack([member[column] for member in results]) for column in range(3)))
    positions = jnp.arange(N_TM * N_HEIGHT, dtype=jnp.int32)
    log_totals, deltas, query_grads = lax.map(first_pass, positions)
    stats_margin = ((1, 1), (1, 1), (0, 0), (0, 0), (0, 0))
    totals_wide = jnp.pad(log_totals.reshape(N_TM, N_HEIGHT, WIDTH_TILES, HEADS, TILE), stats_margin)
    deltas_wide = jnp.pad(deltas.reshape(N_TM, N_HEIGHT, WIDTH_TILES, HEADS, TILE), stats_margin)

    def second_pass(position):
        frame_tile = position // N_HEIGHT
        row_tile = position % N_HEIGHT
        near_queries = window(queries_wide, frame_tile, row_tile)
        near_grads = window(grads_wide, frame_tile, row_tile)
        near_totals = window(totals_wide, frame_tile, row_tile)
        near_deltas = window(deltas_wide, frame_tile, row_tile)
        own_keys = k_norm[frame_tile, row_tile]
        own_values = values[frame_tile, row_tile]
        key_list = []
        value_list = []
        for width_tile in range(WIDTH_TILES):
            start_w = max(0, width_tile - 1)
            stop_w = min(WIDTH_TILES, width_tile + 2)
            span_queries = near_queries[:, :, start_w:stop_w].reshape(-1, HEADS, HEAD_DIM)
            span_grads = near_grads[:, :, start_w:stop_w].reshape(-1, HEADS, HEAD_DIM)
            span_totals = near_totals[:, :, start_w:stop_w].transpose(3, 0, 1, 2, 4).reshape(HEADS, -1)
            span_deltas = near_deltas[:, :, start_w:stop_w].transpose(3, 0, 1, 2, 4).reshape(HEADS, -1)
            allowed = allowed_mask(frame_tile, row_tile, stop_w - start_w)
            key_grad, value_grad = key_side(own_keys[width_tile], own_values[width_tile], span_queries, span_grads, span_totals, span_deltas, allowed, score_scale)
            key_list.append(key_grad)
            value_list.append(value_grad)
        return (jnp.stack(key_list), jnp.stack(value_list))
    key_grads, value_grads = lax.map(second_pass, positions)
    tile_shape = (N_TM, N_HEIGHT, WIDTH_TILES, TILE, HEADS, HEAD_DIM)
    q_tiles, q_terms = norm_back(query_grads.reshape(tile_shape), q_unit, q_inverse, q_gain)
    k_tiles, k_terms = norm_back(key_grads.reshape(tile_shape), k_unit, k_inverse, k_gain)
    factor = 1.0 / math.sqrt(FRAMES * ROWS * COLS * HEADS)
    v_tiles = value_grads.reshape(tile_shape).astype(jnp.bfloat16)
    return (from_tiles(q_tiles), from_tiles(k_tiles), from_tiles(v_tiles), q_terms * factor, k_terms * factor)
```

```python
import functools
import math

import jax
import jax.numpy as jnp
from jax import lax
from jax.experimental import pallas as pl
from jax.experimental.pallas import tpu as pltpu
from jax.sharding import PartitionSpec as P

HEAD_DIM = 128
EPS = 1e-06
MASKED = -1e30
NT = (((1,), (1,)), ((), ()))
NN = (((1,), (0,)), ((), ()))
f32 = jnp.float32
bf16 = jnp.bfloat16


def dot(a, b, dims):
    return lax.dot_general(a, b, dims, preferred_element_type=f32)


def unit_of(raw):
    values = raw.astype(f32)
    inverse = lax.rsqrt(jnp.mean(values * values, axis=-1, keepdims=True) + EPS)
    return values * inverse, inverse


def stack_kernel(raw_ref, other_ref, gain_ref, out_ref):
    for h in range(raw_ref.shape[-1] // HEAD_DIM):
        cols = slice(h * HEAD_DIM, (h + 1) * HEAD_DIM)
        unit, _ = unit_of(raw_ref[:, cols])
        out_ref[0, :, cols] = (unit * gain_ref[...]).astype(bf16)
        out_ref[1, :, cols] = other_ref[:, cols]


def norm_stack(raw, other, gain):
    tokens, channels = raw.shape
    return pl.pallas_call(
        stack_kernel,
        out_shape=jax.ShapeDtypeStruct((2, tokens, channels), bf16),
        name="norm_stack",
    )(raw, other, gain)


def query_kernel(scale, raw_ref, gain_ref, kgain_ref, bias_ref, qg_ref, *refs):
    tiles, (grad_ref, stats_ref, keys, values, columns, sums) = refs[:9], refs[9:]
    h = pl.program_id(0)
    tile = raw_ref.shape[0]
    for i, ref in enumerate(tiles):
        keys[i * tile : (i + 1) * tile, :] = ref[0]
        values[i * tile : (i + 1) * tile, :] = ref[1]
    qn, grads = qg_ref[0], qg_ref[1]
    scores = dot(qn, keys[...], NT) * scale + bias_ref[...]
    highest = jnp.max(scores, axis=-1, keepdims=True)
    terms = jnp.exp(scores - highest)
    total = jnp.sum(terms, axis=-1, keepdims=True)
    prob = terms * (1.0 / total)
    out = dot(prob.astype(bf16), values[...], NN).astype(bf16)
    delta = jnp.sum(grads.astype(f32) * out.astype(f32), axis=-1, keepdims=True)
    prob_grad = dot(grads, values[...], NT)
    score_grad = (prob * (prob_grad - delta)).astype(bf16)
    grad_norm = dot(score_grad, keys[...], NN) * scale
    unit, inverse = unit_of(raw_ref[...])
    g = grad_norm * gain_ref[...]
    inner = jnp.mean(g * unit, axis=-1, keepdims=True)
    grad_ref[...] = ((g - unit * inner) * inverse).astype(bf16)
    terms_q = jnp.sum(grad_norm * unit, axis=0, keepdims=True)
    log_total = highest + jnp.log(total)
    lane = lax.broadcasted_iota(jnp.int32, (tile, HEAD_DIM), 1)

    @pl.when(h == 0)
    def _():
        columns[...] = jnp.zeros_like(columns)
        sums[...] = jnp.zeros_like(sums)

    columns[...] = jnp.where(
        lane == 2 * h, log_total, jnp.where(lane == 2 * h + 1, delta, columns[...])
    )
    sums[...] += terms_q

    @pl.when(h == pl.num_programs(0) - 1)
    def _():
        stats_ref[...] = columns[...].T[:8]
        stats_ref[6:7, 0:HEAD_DIM] = sums[...]
        stats_ref[7:8, 0:HEAD_DIM] = sums[...] * gain_ref[...] / kgain_ref[...]


def query_side(raw, gain, kgain, bias, qg, tiles, scale):
    tile, channels = raw.shape
    heads = channels // HEAD_DIM
    span = 9 * tile
    pair = pl.BlockSpec((2, tile, HEAD_DIM), lambda h: (0, 0, h))
    flat = pl.BlockSpec((tile, HEAD_DIM), lambda h: (0, h))
    whole = lambda a: pl.BlockSpec(a.shape, lambda h: (0,) * a.ndim)
    return pl.pallas_call(
        functools.partial(query_kernel, scale),
        grid=(heads,),
        in_specs=[flat, whole(gain), whole(kgain), whole(bias), pair] + [pair] * 9,
        out_specs=[flat, pl.BlockSpec((8, tile), lambda h: (0, 0))],
        out_shape=[
            jax.ShapeDtypeStruct((tile, channels), bf16),
            jax.ShapeDtypeStruct((8, tile), f32),
        ],
        scratch_shapes=[
            pltpu.VMEM((span, HEAD_DIM), bf16),
            pltpu.VMEM((span, HEAD_DIM), bf16),
            pltpu.VMEM((tile, HEAD_DIM), f32),
            pltpu.VMEM((1, HEAD_DIM), f32),
        ],
        compiler_params=pltpu.CompilerParams(vmem_limit_bytes=40 * 2**20),
        cost_estimate=pl.CostEstimate(
            flops=8 * tile * span * channels,
            bytes_accessed=24 * tile * channels * 2,
            transcendentals=tile * span * heads,
        ),
        name="query_side",
    )(raw, gain, kgain, bias, qg, *tiles)


def key_kernel(scale, raw_ref, gain_ref, bias_ref, stats_ref, kv_ref, *refs):
    tiles, (kgrad_ref, vgrad_ref, queries, grads) = refs[:9], refs[9:]
    h = pl.program_id(0)
    tile = raw_ref.shape[0]
    for i, ref in enumerate(tiles):
        queries[i * tile : (i + 1) * tile, :] = ref[0]
        grads[i * tile : (i + 1) * tile, :] = ref[1]
    log_total = stats_ref[pl.ds(2 * h, 1), :]
    delta = stats_ref[pl.ds(2 * h + 1, 1), :]
    scores = dot(kv_ref[0], queries[...], NT) * scale
    prob = jnp.exp(scores + (bias_ref[...] - log_total))
    vgrad_ref[...] = dot(prob.astype(bf16), grads[...], NN).astype(bf16)
    prob_grad = dot(kv_ref[1], grads[...], NT)
    score_grad = (prob * (prob_grad - delta)).astype(bf16)
    grad_norm = dot(score_grad, queries[...], NN) * scale
    unit, inverse = unit_of(raw_ref[...])
    g = grad_norm * gain_ref[...]
    inner = jnp.mean(g * unit, axis=-1, keepdims=True)
    kgrad_ref[...] = ((g - unit * inner) * inverse).astype(bf16)


def key_side(raw, gain, bias, stats, kv, tiles, scale):
    tile, channels = raw.shape
    heads = channels // HEAD_DIM
    span = 9 * tile
    pair = pl.BlockSpec((2, tile, HEAD_DIM), lambda h: (0, 0, h))
    flat = pl.BlockSpec((tile, HEAD_DIM), lambda h: (0, h))
    whole = lambda a: pl.BlockSpec(a.shape, lambda h: (0,) * a.ndim)
    return pl.pallas_call(
        functools.partial(key_kernel, scale),
        grid=(heads,),
        in_specs=[flat, whole(gain), whole(bias), whole(stats), pair] + [pair] * 9,
        out_specs=[flat, flat],
        out_shape=[jax.ShapeDtypeStruct((tile, channels), bf16)] * 2,
        scratch_shapes=[pltpu.VMEM((span, HEAD_DIM), bf16)] * 2,
        compiler_params=pltpu.CompilerParams(vmem_limit_bytes=40 * 2**20),
        cost_estimate=pl.CostEstimate(
            flops=8 * tile * span * channels,
            bytes_accessed=24 * tile * channels * 2,
            transcendentals=tile * span * heads,
        ),
        name="key_side",
    )(raw, gain, bias, stats, kv, *tiles)


def swap(x, axis):
    n = lax.axis_size(axis)
    return lax.ppermute(x, axis, [(i, i ^ 1) for i in range(n)])


def hop(x, axis):
    n = lax.axis_size(axis)
    route = [(i, i + 2) for i in range(0, n - 2, 2)] + [(i, i - 2) for i in range(3, n, 2)]
    return lax.ppermute(x, axis, route)


def column(x):
    mate = swap(x, "tm")
    return [x, mate, hop(mate, "tm")]


def halo(x):
    mate = swap(x, "height")
    own = column(x)
    beyond = hop(mate, "height")
    return own + column(mate) + column(beyond)


def outside(axis):
    at, n = lax.axis_index(axis), lax.axis_size(axis)
    return (at == 0) | (at == n - 1)


def mask_bias(tile):
    slot = lax.broadcasted_iota(jnp.int32, (1, 9 * tile), 1) // tile
    gone = (outside("height") & (slot >= 6)) | (outside("tm") & (slot % 3 == 2))
    return jnp.where(gone, MASKED, 0.0).astype(f32)


def gather_stats(stats):
    axes = ("tm", "height")
    n_tm, n_h = (lax.axis_size(a) for a in axes)
    n = n_tm * n_h
    sent = jnp.broadcast_to(stats[None], (n,) + stats.shape)
    got = lax.all_to_all(sent, axes, 0, 0)
    sums = jnp.sum(got[:, 6:8, :HEAD_DIM], axis=0)

    def places(axis, size):
        at = lax.axis_index(axis)
        mate = at ^ 1
        beyond = jnp.clip(2 * at - mate, 0, size - 1)
        return at, mate, beyond

    rows, frames = places("height", n_h), places("tm", n_tm)
    index = jnp.stack([t * n_h + r for r in rows for t in frames])
    near = jnp.take(got[:, :6], index, axis=0)
    return near.transpose(1, 0, 2).reshape(6, -1), sums


def shards(q_raw, k_raw, value_in, out_grad, q_gain, k_gain):
    shape = q_raw.shape
    channels = shape[-1]
    tile = math.prod(shape[:-1])
    scale = 1.0 / math.sqrt(HEAD_DIM)
    q, k, v, do = (a.reshape(tile, channels) for a in (q_raw, k_raw, value_in, out_grad))
    qg_gain, kg_gain = q_gain.reshape(1, HEAD_DIM), k_gain.reshape(1, HEAD_DIM)
    bias = mask_bias(tile)
    kv = norm_stack(k, v, kg_gain)
    kv_tiles = halo(kv)
    qg = norm_stack(q, do, qg_gain)
    qg_tiles = halo(qg)
    q_out, stats = query_side(q, qg_gain, kg_gain, bias, qg, kv_tiles, scale)
    near, sums = gather_stats(stats)
    k_out, v_out = key_side(k, kg_gain, bias, near, kv, qg_tiles, scale)
    total = sums
    for step in (1, 2):
        n = lax.axis_size("heads")
        total = total + lax.ppermute(total, "heads", [(i, i ^ step) for i in range(n)])
    count = tile * (channels // HEAD_DIM)
    for axis in ("tm", "height", "heads"):
        count *= lax.axis_size(axis)
    total = total / math.sqrt(count)
    return (
        q_out.reshape(shape),
        k_out.reshape(shape),
        v_out.reshape(shape),
        total[0],
        total[1],
    )


def solution(mesh):
    split = P("tm", "height", None, "heads")
    return jax.shard_map(
        shards,
        mesh=mesh,
        in_specs=(split, split, split, split, P(), P()),
        out_specs=(split, split, split, P(), P()),
        check_vma=False,
    )
```

```python
import functools
import math

import jax
import jax.numpy as jnp
from jax import lax
from jax.experimental import pallas as pl
from jax.experimental.pallas import tpu as pltpu
from jax.sharding import PartitionSpec as P

HEAD_DIM = 128
EPS = 1e-06
MASKED = -1e30
NT = (((1,), (1,)), ((), ()))
NN = (((1,), (0,)), ((), ()))
TN = (((0,), (0,)), ((), ()))
f32 = jnp.float32
bf16 = jnp.bfloat16
COST = pl.CostEstimate(flops=10**6, bytes_accessed=10**5, transcendentals=0)


def dot(a, b, dims):
    return lax.dot_general(a, b, dims, preferred_element_type=f32)


def unit_of(raw):
    values = raw.astype(f32)
    inverse = lax.rsqrt(jnp.mean(values * values, axis=-1, keepdims=True) + EPS)
    return values * inverse, inverse


def stack_kernel(raw_ref, other_ref, gain_ref, out_ref):
    tokens = out_ref.shape[2]
    for h in range(raw_ref.shape[-1] // HEAD_DIM):
        cols = slice(h * HEAD_DIM, (h + 1) * HEAD_DIM)
        unit, _ = unit_of(raw_ref[..., cols].reshape(tokens, HEAD_DIM))
        out_ref[0, 0, :, cols] = (unit * gain_ref[...]).astype(bf16)
        out_ref[0, 1, :, cols] = other_ref[..., cols].reshape(tokens, HEAD_DIM)


def norm_stack(raw, other, gain):
    tokens, channels = math.prod(raw.shape[:-1]), raw.shape[-1]
    return pl.pallas_call(
        stack_kernel,
        out_shape=jax.ShapeDtypeStruct((1, 2, tokens, channels), bf16),
        cost_estimate=COST,
        name="norm_stack",
    )(raw, other, gain)


def fill(tiles, first, second):
    at = 0
    for ref in tiles:
        rows, _, tile, _ = ref.shape
        for r in range(rows):
            first[at : at + tile, :] = ref[r, 0]
            second[at : at + tile, :] = ref[r, 1]
            at += tile


def query_kernel(scale, q_ref, qg_ref, qgain_ref, kgain_ref, bias_ref, *refs):
    tiles, (qgrad_ref, sums_ref, stats_ref) = refs[:9], refs[9:12]
    keys, values, columns = refs[12:]
    h = pl.program_id(0)
    tile = qg_ref.shape[2]
    fill(tiles, keys, values)
    qn, grads = qg_ref[0, 0], qg_ref[0, 1]
    scores = dot(qn, keys[...], NT) * scale + bias_ref[...]
    highest = jnp.max(scores, axis=-1, keepdims=True)
    terms = jnp.exp(scores - highest)
    total = jnp.sum(terms, axis=-1, keepdims=True)
    prob = terms * (1.0 / total)
    out = dot(prob.astype(bf16), values[...], NN).astype(bf16)
    delta = jnp.sum(grads.astype(f32) * out.astype(f32), axis=-1, keepdims=True)
    prob_grad = dot(grads, values[...], NT)
    score_grad = (prob * (prob_grad - delta)).astype(bf16)
    grad_norm = dot(score_grad, keys[...], NN) * scale
    unit, inverse = unit_of(q_ref[...].reshape(tile, HEAD_DIM))
    g = grad_norm * qgain_ref[...]
    inner = jnp.mean(g * unit, axis=-1, keepdims=True)
    qgrad = ((g - unit * inner) * inverse).astype(bf16)
    qgrad_ref[...] = qgrad.reshape(qgrad_ref.shape)
    q_terms = jnp.sum(grad_norm * unit, axis=0, keepdims=True)
    k_terms = jnp.sum(grad_norm * qn.astype(f32), axis=0, keepdims=True)
    log_total = highest + jnp.log(total)
    lane = lax.broadcasted_iota(jnp.int32, (tile, HEAD_DIM), 1)

    @pl.when(h == 0)
    def _():
        columns[...] = jnp.zeros_like(columns)
        sums_ref[...] = jnp.zeros_like(sums_ref)

    columns[...] = jnp.where(
        lane == 2 * h, log_total, jnp.where(lane == 2 * h + 1, delta, columns[...])
    )
    sums_ref[0:1] += q_terms
    sums_ref[1:2] += k_terms / kgain_ref[...]

    @pl.when(h == pl.num_programs(0) - 1)
    def _():
        stats_ref[...] = columns[...].T[:8]


def key_kernel(scale, bias_ref, *refs):
    stats, queries_in, keys_in = refs[:3], refs[3:6], refs[6:9]
    own_ref, outs = refs[9], refs[10:12]
    queries, grads, keys, values = refs[12:]
    h = pl.program_id(0)
    tile = own_ref.shape[1]
    fill(queries_in, queries, grads)
    fill(keys_in, keys, values)

    def row(at):
        return jnp.concatenate([ref[pl.ds(at, 1), :] for ref in stats], axis=1)

    scores = dot(keys[...], queries[...], NT) * scale
    prob = jnp.exp(scores + (bias_ref[...] - row(2 * h)))
    value_terms = dot(prob.astype(bf16), grads[...], NN)
    prob_grad = dot(values[...], grads[...], NT)
    score_grad = (prob * (prob_grad - row(2 * h + 1))).astype(bf16)
    key_terms = dot(score_grad, queries[...], NN) * scale
    own_ref[0] = key_terms[:tile]
    own_ref[1] = value_terms[:tile]
    for i, ref in enumerate(outs):
        rows = slice((i + 1) * tile, (i + 2) * tile)
        ref[0, 0] = key_terms[rows].astype(bf16)
        ref[0, 1] = value_terms[rows].astype(bf16)


def column(a):
    first = (0,) * (len(a.shape) - 1)
    return pl.BlockSpec(a.shape[:-1] + (HEAD_DIM,), lambda h: first + (h,))


def whole(a):
    return pl.BlockSpec(a.shape, lambda h: (0,) * len(a.shape))


def query_side(q, qg, qgain, kgain, bias, tiles, scale):
    _, _, tile, channels = qg.shape
    span = len(tiles) * tile
    qgrad = jax.ShapeDtypeStruct(q.shape, bf16)
    sums = jax.ShapeDtypeStruct((2, HEAD_DIM), f32)
    stats = jax.ShapeDtypeStruct((8, tile), f32)
    return pl.pallas_call(
        functools.partial(query_kernel, scale),
        grid=(channels // HEAD_DIM,),
        in_specs=[column(q), column(qg), whole(qgain), whole(kgain), whole(bias)]
        + [column(t) for t in tiles],
        out_specs=[column(qgrad), whole(sums), whole(stats)],
        out_shape=[qgrad, sums, stats],
        scratch_shapes=[
            pltpu.VMEM((span, HEAD_DIM), bf16),
            pltpu.VMEM((span, HEAD_DIM), bf16),
            pltpu.VMEM((tile, HEAD_DIM), f32),
        ],
        compiler_params=pltpu.CompilerParams(vmem_limit_bytes=40 * 2**20),
        cost_estimate=COST,
        name="query_side",
    )(q, qg, qgain, kgain, bias, *tiles)


def key_side(bias, stats, queries, keys, scale):
    _, _, tile, channels = keys[0].shape
    span = len(keys) * tile
    own = jax.ShapeDtypeStruct((2, tile, channels), f32)
    sent = jax.ShapeDtypeStruct((1, 2, tile, channels), bf16)
    return pl.pallas_call(
        functools.partial(key_kernel, scale),
        grid=(channels // HEAD_DIM,),
        in_specs=[whole(bias)]
        + [whole(a) for a in stats]
        + [column(t) for t in queries + keys],
        out_specs=[column(own), column(sent), column(sent)],
        out_shape=[own, sent, sent],
        scratch_shapes=[pltpu.VMEM((span, HEAD_DIM), bf16)] * 4,
        compiler_params=pltpu.CompilerParams(vmem_limit_bytes=40 * 2**20),
        cost_estimate=COST,
        name="key_side",
    )(bias, *stats, *queries, *keys)


def finish_kernel(k_ref, gain_ref, own_ref, mate_ref, kgrad_ref, vgrad_ref):
    tokens, part = own_ref.shape[1], k_ref.shape[:-1] + (HEAD_DIM,)
    for h in range(k_ref.shape[-1] // HEAD_DIM):
        cols = slice(h * HEAD_DIM, (h + 1) * HEAD_DIM)
        total = [own_ref[i, :, cols] + mate_ref[0, i, :, cols].astype(f32) for i in range(2)]
        vgrad_ref[..., cols] = total[1].astype(bf16).reshape(part)
        unit, inverse = unit_of(k_ref[..., cols].reshape(tokens, HEAD_DIM))
        g = total[0] * gain_ref[...]
        inner = jnp.mean(g * unit, axis=-1, keepdims=True)
        kgrad = ((g - unit * inner) * inverse).astype(bf16)
        kgrad_ref[..., cols] = kgrad.reshape(part)


def finish(k, gain, own, mate):
    return pl.pallas_call(
        finish_kernel,
        out_shape=[jax.ShapeDtypeStruct(k.shape, bf16)] * 2,
        cost_estimate=COST,
        name="finish",
    )(k, gain, own, mate)


def swapped(x, axis, bits):
    n = lax.axis_size(axis)
    return lax.ppermute(x, axis, [(i, i ^ bits) for i in range(n)])


def swap(x, axis):
    return swapped(x, axis, 1)


def hops(n, back=False):
    route = [(i, i + 2 - 4 * (i % 2)) for i in range(n)]
    return [(j, i) if back else (i, j) for i, j in route if 0 <= j < n]


def hop(x, axis, back=False):
    return lax.ppermute(x, axis, hops(lax.axis_size(axis), back))


def hop_both(x):
    n_tm, n_h = lax.axis_size("tm"), lax.axis_size("height")
    route = [(a * n_h + b, c * n_h + d) for a, c in hops(n_tm) for b, d in hops(n_h)]
    return lax.ppermute(x, ("tm", "height"), route)


def level(total, axis, other, bits, other_bits):
    if axis == other:
        far = swapped(total, axis, bits ^ other_bits)
    else:
        n, m = lax.axis_size(axis), lax.axis_size(other)
        route = [
            (i * m + j, (i ^ bits) * m + (j ^ other_bits)) for i in range(n) for j in range(m)
        ]
        far = lax.ppermute(total, (axis, other), route)
    return (total + swapped(total, axis, bits)) + (swapped(total, other, other_bits) + far)


def together(steps, like, *args):
    always = lax.optimization_barrier(jnp.bool_(True))
    return lax.cond(always, steps, lambda *_: like, *args)


def frames(kv, qg):
    c, d = swap(kv, "tm"), swap(qg, "tm")
    return c, d, hop(c, "tm"), hop(d, "tm")


def last_levels(sums):
    sums = level(sums, "tm", "tm", 2, 4)
    return level(sums, "height", "height", 2, 4)


def plus(a, b):
    return (a.astype(f32) + b.astype(f32)).astype(bf16)


def outside(axis):
    at, n = lax.axis_index(axis), lax.axis_size(axis)
    return (at == 0) | (at == n - 1)


def mask_bias(tile, rows):
    each = 3 if rows else 1
    slot = lax.broadcasted_iota(jnp.int32, (1, 3 * each * tile), 1) // tile
    gone = outside("tm") & (slot >= 2 * each)
    if rows:
        gone |= outside("height") & (slot % 3 == 2)
    return jnp.where(gone, MASKED, 0.0).astype(f32)


def with_sums(stats, sums):
    return stats.at[6:8, :HEAD_DIM].set(sums)


def shards(q_raw, k_raw, value_in, out_grad, q_gain, k_gain):
    shape = q_raw.shape
    channels = shape[-1]
    tile = math.prod(shape[:-1])
    scale = 1.0 / math.sqrt(HEAD_DIM)
    qg_gain, kg_gain = q_gain.reshape(1, HEAD_DIM), k_gain.reshape(1, HEAD_DIM)

    kv = norm_stack(k_raw, value_in, kg_gain)
    z = swap(kv, "height")
    qg = norm_stack(q_raw, out_grad, qg_gain)
    c0, d0, y0, w0 = together(frames, (kv, qg, kv, qg), kv, qg)
    z, c0, d0, y0, w0 = lax.optimization_barrier((z, c0, d0, y0, w0))
    c1 = swap(z, "tm")
    x, xy, y1 = hop(z, "height"), hop_both(c1), hop(c1, "tm")
    x, xy, y1 = lax.optimization_barrier((x, xy, y1))
    c2 = swap(x, "tm")
    tiles = [kv, z, x, c0, c1, c2, y0, y1, xy]
    q_out, sums, stats = query_side(
        q_raw, qg, qg_gain, kg_gain, mask_bias(tile, True), tiles, scale
    )

    c_stats = swap(with_sums(stats, sums), "tm")
    sums = sums + c_stats[6:8, :HEAD_DIM]
    y_stats = hop(c_stats, "tm")
    sums = sums + swap(sums, "height")
    y_stats, sums = lax.optimization_barrier((y_stats, sums))
    own, pz, px = key_side(
        mask_bias(tile, False), [stats, c_stats, y_stats], [qg, d0, w0], [kv, z, x], scale
    )
    px, sums = lax.optimization_barrier((px, sums))
    pz = plus(pz, hop(px, "height", True))
    sums = level(sums, "heads", "heads", 1, 2)
    pz, sums = lax.optimization_barrier((pz, sums))
    pz = swap(pz, "height")
    total = together(last_levels, sums, sums)
    pz, total = lax.optimization_barrier((pz, total))
    k_out, v_out = finish(k_raw, kg_gain, own, pz)
    count = tile * (channels // HEAD_DIM)
    for axis in ("tm", "height", "heads"):
        count *= lax.axis_size(axis)
    total = total / math.sqrt(count)
    return (
        q_out,
        k_out,
        v_out,
        total[0],
        total[1],
    )


def solution(mesh):
    split = P("tm", "height", None, "heads")
    return jax.shard_map(
        shards,
        mesh=mesh,
        in_specs=(split, split, split, split, P(), P()),
        out_specs=(split, split, split, P(), P()),
        check_vma=False,
    )
```

```python
import functools
import math

import jax
import jax.numpy as jnp
from jax import lax
from jax.experimental import pallas as pl
from jax.experimental.pallas import tpu as pltpu
from jax.sharding import PartitionSpec as P

HEAD_DIM = 128
EPS = 1e-06
MASKED = -1e30
NT = (((1,), (1,)), ((), ()))
NN = (((1,), (0,)), ((), ()))
TN = (((0,), (0,)), ((), ()))
f32 = jnp.float32
bf16 = jnp.bfloat16
COST = pl.CostEstimate(flops=10**6, bytes_accessed=10**5, transcendentals=0)


def dot(a, b, dims):
    return lax.dot_general(a, b, dims, preferred_element_type=f32)


def unit_of(raw):
    values = raw.astype(f32)
    inverse = lax.rsqrt(jnp.mean(values * values, axis=-1, keepdims=True) + EPS)
    return values * inverse, inverse


def head_cols(channels):
    return [slice(at, at + HEAD_DIM) for at in range(0, channels, HEAD_DIM)]


def stack_kernel(raw_ref, other_ref, gain_ref, *refs):
    flat_in, out_ref, flat_out = refs[: len(refs) // 2], refs[len(refs) // 2], refs[len(refs) // 2 + 1 :]
    tokens = out_ref.shape[2]
    for cols in head_cols(raw_ref.shape[-1]):
        unit, _ = unit_of(raw_ref[..., cols].reshape(tokens, HEAD_DIM))
        out_ref[0, 0, :, cols] = (unit * gain_ref[...]).astype(bf16)
        out_ref[0, 1, :, cols] = other_ref[..., cols].reshape(tokens, HEAD_DIM)
        for ref, flat_ref in zip(flat_in, flat_out):
            flat_ref[:, cols] = ref[..., cols].reshape(tokens, HEAD_DIM)


def norm_stack(raw, other, gain, *flat):
    tokens, channels = math.prod(raw.shape[:-1]), raw.shape[-1]
    return pl.pallas_call(
        stack_kernel,
        out_shape=[jax.ShapeDtypeStruct((1, 2, tokens, channels), bf16)]
        + [jax.ShapeDtypeStruct((tokens, channels), bf16) for _ in flat],
        cost_estimate=COST,
        name="norm_stack",
    )(raw, other, gain, *flat)


def fill(tiles, first, second):
    tile = tiles[0].shape[2]
    for i, ref in enumerate(tiles):
        rows = slice(i * tile, (i + 1) * tile)
        first[rows, :] = ref[0, 0]
        second[rows, :] = ref[0, 1]


def norm_back(grad_norm, raw, gain):
    unit, inverse = unit_of(raw)
    g = grad_norm * gain
    inner = jnp.mean(g * unit, axis=-1, keepdims=True)
    return ((g - unit * inner) * inverse).astype(bf16), unit


def query_kernel(scale, q_ref, qg_ref, qgain_ref, kgain_ref, bias_ref, *refs):
    tiles, (qgrad_ref, sums_ref, stats_ref), (keys, values) = refs[:9], refs[9:12], refs[12:]
    _, _, tile, channels = qg_ref.shape
    heads = head_cols(channels)
    fill(tiles, keys, values)
    lane = lax.broadcasted_iota(jnp.int32, (tile, HEAD_DIM), 1)
    columns = jnp.zeros((tile, HEAD_DIM), f32)
    q_terms = k_terms = jnp.zeros((1, HEAD_DIM), f32)
    scores = [
        dot(qg_ref[0, 0, :, cols], keys[:, cols], NT) * scale + bias_ref[...] for cols in heads
    ]
    prob_grads = [dot(qg_ref[0, 1, :, cols], values[:, cols], NT) for cols in heads]
    probs = []
    for h, cols in enumerate(heads):
        highest = jnp.max(scores[h], axis=-1, keepdims=True)
        terms = jnp.exp(scores[h] - highest)
        total = jnp.sum(terms, axis=-1, keepdims=True)
        probs.append(terms * (1.0 / total))
        columns = jnp.where(lane == 2 * h, highest + jnp.log(total), columns)
    outs = [dot(probs[h].astype(bf16), values[:, cols], NN).astype(bf16) for h, cols in enumerate(heads)]
    grads = []
    for h, cols in enumerate(heads):
        products = qg_ref[0, 1, :, cols].astype(f32) * outs[h].astype(f32)
        delta = jnp.sum(products, axis=-1, keepdims=True)
        columns = jnp.where(lane == 2 * h + 1, delta, columns)
        score_grad = (probs[h] * (prob_grads[h] - delta)).astype(bf16)
        grads.append(dot(score_grad, keys[:, cols], NN) * scale)
    for h, cols in enumerate(heads):
        qgrad_ref[:, cols], unit = norm_back(grads[h], q_ref[:, cols], qgain_ref[...])
        qn = qg_ref[0, 0, :, cols].astype(f32)
        q_terms += jnp.sum(grads[h] * unit, axis=0, keepdims=True)
        k_terms += jnp.sum(grads[h] * qn, axis=0, keepdims=True)
    sums_ref[0:1] = q_terms
    sums_ref[1:2] = k_terms / kgain_ref[...]
    stats_ref[...] = columns.T[:8]


def key_kernel(scale, n, bias_ref, *refs):
    stats, queries_in, keys_in = refs[:3], refs[3:6], refs[6 : 6 + n]
    outs, (queries, grads, keys, values) = refs[6 + n : -4], refs[-4:]
    _, _, tile, channels = queries_in[0].shape
    heads = head_cols(channels)
    fill(queries_in, queries, grads)
    fill(keys_in, keys, values)
    rows = jnp.concatenate([ref[...] for ref in stats], axis=1)
    scores = [dot(keys[:, cols], queries[:, cols], NT) * scale for cols in heads]
    prob_grads = [dot(values[:, cols], grads[:, cols], NT) for cols in heads]
    for h, cols in enumerate(heads):
        prob = jnp.exp(scores[h] + (bias_ref[...] - rows[2 * h : 2 * h + 1]))
        value_terms = dot(prob.astype(bf16), grads[:, cols], NN)
        score_grad = (prob * (prob_grads[h] - rows[2 * h + 1 : 2 * h + 2])).astype(bf16)
        key_terms = dot(score_grad, queries[:, cols], NN) * scale
        for i, ref in enumerate(outs):
            part = slice(i * tile, (i + 1) * tile)
            ref[0, 0, :, cols] = key_terms[part].astype(ref.dtype)
            ref[0, 1, :, cols] = value_terms[part].astype(ref.dtype)


def query_side(q, qg, qgain, kgain, bias, tiles, scale):
    _, _, tile, channels = qg.shape
    span = len(tiles) * tile
    qgrad = jax.ShapeDtypeStruct(q.shape, bf16)
    sums = jax.ShapeDtypeStruct((2, HEAD_DIM), f32)
    stats = jax.ShapeDtypeStruct((8, tile), f32)
    return pl.pallas_call(
        functools.partial(query_kernel, scale),
        out_shape=[qgrad, sums, stats],
        scratch_shapes=[
            pltpu.VMEM((span, channels), bf16),
            pltpu.VMEM((span, channels), bf16),
        ],
        compiler_params=pltpu.CompilerParams(vmem_limit_bytes=40 * 2**20),
        cost_estimate=COST,
        name="query_side",
    )(q, qg, qgain, kgain, bias, *tiles)


def key_side(bias, stats, queries, keys, types, scale):
    shape = keys[0].shape
    _, _, tile, channels = shape
    held = [pltpu.VMEM((n * tile, channels), bf16) for n in (3, 3, len(keys), len(keys))]
    return pl.pallas_call(
        functools.partial(key_kernel, scale, len(keys)),
        out_shape=[jax.ShapeDtypeStruct(shape, t) for t in types],
        scratch_shapes=held,
        compiler_params=pltpu.CompilerParams(vmem_limit_bytes=40 * 2**20),
        cost_estimate=COST,
        name="key_side",
    )(bias, *stats, *queries, *keys)


def finish_kernel(k_ref, gain_ref, own_ref, mate_ref, kgrad_ref, vgrad_ref):
    part = kgrad_ref.shape[:-1] + (HEAD_DIM,)
    for cols in head_cols(k_ref.shape[-1]):
        total = [own_ref[0, i, :, cols] + mate_ref[0, i, :, cols].astype(f32) for i in range(2)]
        vgrad_ref[..., cols] = total[1].astype(bf16).reshape(part)
        kgrad, _ = norm_back(total[0], k_ref[:, cols], gain_ref[...])
        kgrad_ref[..., cols] = kgrad.reshape(part)


def finish(k, gain, own, mate, shape):
    return pl.pallas_call(
        finish_kernel,
        out_shape=[jax.ShapeDtypeStruct(shape, bf16)] * 2,
        cost_estimate=pl.CostEstimate(flops=10**6, bytes_accessed=2**22, transcendentals=0),
        name="finish",
    )(k, gain, own, mate)


def swapped(x, axis, bits):
    n = lax.axis_size(axis)
    return lax.ppermute(x, axis, [(i, i ^ bits) for i in range(n)])


def swap(x, axis):
    return swapped(x, axis, 1)


def rows_route(n, back=False):
    route = [(i, i + 2 - 4 * (i % 2)) for i in range(n)]
    return [(j, i) if back else (i, j) for i, j in route if 0 <= j < n]


def frames_route(n):
    return [(i, j) for i in range(n) for j in [i - 1 + 2 * (i % 2)] if 0 <= j < n]


def hop(x, back=False):
    return lax.ppermute(x, "height", rows_route(lax.axis_size("height"), back))


def far(x):
    return lax.ppermute(x, "tm", frames_route(lax.axis_size("tm")))


def hop_far(x):
    n_tm, n_h = lax.axis_size("tm"), lax.axis_size("height")
    route = [
        (a * n_h + b, c * n_h + d) for a, c in frames_route(n_tm) for b, d in rows_route(n_h)
    ]
    return lax.ppermute(x, ("tm", "height"), route)


def level(total, axis, other, bits, other_bits):
    if axis == other:
        far = swapped(total, axis, bits ^ other_bits)
    else:
        n, m = lax.axis_size(axis), lax.axis_size(other)
        route = [
            (i * m + j, (i ^ bits) * m + (j ^ other_bits)) for i in range(n) for j in range(m)
        ]
        far = lax.ppermute(total, (axis, other), route)
    return (total + swapped(total, axis, bits)) + (swapped(total, other, other_bits) + far)


def together(steps, like, *args):
    always = lax.optimization_barrier(jnp.bool_(True))
    return lax.cond(always, steps, lambda *_: like, *args)


def frames(kv, qg):
    return swap(kv, "tm"), swap(qg, "tm"), far(kv), far(qg)


def last_levels(sums):
    n_tm, n_h = lax.axis_size("tm"), lax.axis_size("height")
    groups = [
        [t * n_h + r for t in range(a, n_tm, 2) for r in range(b, n_h, 2)]
        for a in range(2)
        for b in range(2)
    ]
    sent = jnp.broadcast_to(sums[None], (len(groups[0]),) + sums.shape)
    got = lax.all_to_all(sent, ("tm", "height"), 0, 0, axis_index_groups=groups)
    return jnp.sum(got, axis=0)


def after(x, first):
    return lax.optimization_barrier((x, first))[0]


def plus(a, b):
    return (a.astype(f32) + b.astype(f32)).astype(bf16)


def outside(axis):
    at, n = lax.axis_index(axis), lax.axis_size(axis)
    return (at == 0) | (at == n - 1)


def mask_bias(tile, rows):
    each = 3 if rows else 1
    slot = lax.broadcasted_iota(jnp.int32, (1, 3 * each * tile), 1) // tile
    gone = outside("tm") & (slot >= 2 * each)
    if rows:
        gone |= outside("height") & (slot % 3 == 2)
    return jnp.where(gone, MASKED, 0.0).astype(f32)


def with_sums(stats, sums):
    return stats.at[6:8, :HEAD_DIM].set(sums)


def shards(q_raw, k_raw, value_in, out_grad, q_gain, k_gain):
    shape = q_raw.shape
    channels = shape[-1]
    tile = math.prod(shape[:-1])
    scale = 1.0 / math.sqrt(HEAD_DIM)
    qg_gain, kg_gain = q_gain.reshape(1, HEAD_DIM), k_gain.reshape(1, HEAD_DIM)

    (kv,) = norm_stack(k_raw, value_in, kg_gain)
    z = swap(kv, "height")
    qg, q_flat, k_flat = norm_stack(q_raw, out_grad, qg_gain, q_raw, k_raw)
    c0, d0, y0, w0 = together(frames, (kv, qg, kv, qg), kv, qg)
    z, c0, d0, y0, w0 = lax.optimization_barrier((z, c0, d0, y0, w0))
    c1 = swap(z, "tm")
    x, xy, y1 = hop(z), hop_far(z), far(z)
    x, xy, y1, c1 = lax.optimization_barrier((x, xy, y1, c1))
    c2 = swap(x, "tm")
    tiles = [kv, z, x, c0, c1, c2, y0, y1, xy]
    q_out, sums, stats = query_side(
        q_flat, qg, qg_gain, kg_gain, mask_bias(tile, True), tiles, scale
    )

    c_stats = swap(with_sums(stats, sums), "tm")
    sums = sums + c_stats[6:8, :HEAD_DIM]
    y_stats = far(stats)
    sums = level(sums, "heads", "heads", 1, 2)
    near = mask_bias(tile, False), [stats, c_stats, y_stats], [qg, d0, w0]
    (px,) = key_side(*near, [x], [bf16], scale)
    own, pz = key_side(*near, [kv, z], [f32, bf16], scale)
    px, sums = lax.optimization_barrier((px, sums))
    pz = plus(pz, hop(px, True))
    sums = sums + swap(sums, "height")
    pz, sums = lax.optimization_barrier((pz, sums))
    pz = swap(pz, "height")
    total = together(last_levels, sums, sums)
    pz, total = lax.optimization_barrier((pz, total))
    k_out, v_out = finish(k_flat, kg_gain, own, pz, shape)
    count = tile * (channels // HEAD_DIM)
    for axis in ("tm", "height", "heads"):
        count *= lax.axis_size(axis)
    total = total / math.sqrt(count)
    return (
        q_out.reshape(shape),
        k_out,
        v_out,
        total[0],
        total[1],
    )


def solution(mesh):
    split = P("tm", "height", None, "heads")
    return jax.shard_map(
        shards,
        mesh=mesh,
        in_specs=(split, split, split, split, P(), P()),
        out_specs=(split, split, split, P(), P()),
        check_vma=False,
    )
```

```python
import functools
import math

import jax
import jax.numpy as jnp
from jax import lax
from jax.experimental import pallas as pl
from jax.experimental.pallas import tpu as pltpu
from jax.sharding import PartitionSpec as P

HEAD_DIM = 128
EPS = 1e-06
MASKED = -1e30
NT = (((1,), (1,)), ((), ()))
NN = (((1,), (0,)), ((), ()))
TN = (((0,), (0,)), ((), ()))
f32 = jnp.float32
bf16 = jnp.bfloat16
COST = pl.CostEstimate(flops=10**6, bytes_accessed=10**5, transcendentals=0)


def dot(a, b, dims):
    return lax.dot_general(a, b, dims, preferred_element_type=f32)


def unit_of(raw):
    values = raw.astype(f32)
    inverse = lax.rsqrt(jnp.mean(values * values, axis=-1, keepdims=True) + EPS)
    return values * inverse, inverse


def head_cols(channels):
    return [slice(at, at + HEAD_DIM) for at in range(0, channels, HEAD_DIM)]


def stack_kernel(raw_ref, other_ref, gain_ref, *refs):
    flat_in, out_ref, flat_out = refs[: len(refs) // 2], refs[len(refs) // 2], refs[len(refs) // 2 + 1 :]
    tokens = out_ref.shape[2]
    for cols in head_cols(raw_ref.shape[-1]):
        unit, _ = unit_of(raw_ref[..., cols].reshape(tokens, HEAD_DIM))
        out_ref[0, 0, :, cols] = (unit * gain_ref[...]).astype(bf16)
        out_ref[0, 1, :, cols] = other_ref[..., cols].reshape(tokens, HEAD_DIM)
        for ref, flat_ref in zip(flat_in, flat_out):
            flat_ref[:, cols] = ref[..., cols].reshape(tokens, HEAD_DIM)


def norm_stack(raw, other, gain, *flat):
    tokens, channels = math.prod(raw.shape[:-1]), raw.shape[-1]
    return pl.pallas_call(
        stack_kernel,
        out_shape=[jax.ShapeDtypeStruct((1, 2, tokens, channels), bf16)]
        + [jax.ShapeDtypeStruct((tokens, channels), bf16) for _ in flat],
        cost_estimate=COST,
        name="norm_stack",
    )(raw, other, gain, *flat)


def fill(tiles, first, second):
    tile = tiles[0].shape[2]
    for i, ref in enumerate(tiles):
        rows = slice(i * tile, (i + 1) * tile)
        first[rows, :] = ref[0, 0]
        second[rows, :] = ref[0, 1]


def norm_back(grad_norm, raw, gain):
    unit, inverse = unit_of(raw)
    g = grad_norm * gain
    inner = jnp.mean(g * unit, axis=-1, keepdims=True)
    return ((g - unit * inner) * inverse).astype(bf16), unit


def query_kernel(scale, q_ref, qg_ref, qgain_ref, kgain_ref, bias_ref, *refs):
    tiles, (qgrad_ref, sums_ref, stats_ref), (keys, values) = refs[:9], refs[9:12], refs[12:]
    _, _, tile, channels = qg_ref.shape
    heads = head_cols(channels)
    fill(tiles, keys, values)
    lane = lax.broadcasted_iota(jnp.int32, (tile, HEAD_DIM), 1)
    columns = jnp.zeros((tile, HEAD_DIM), f32)
    q_terms = k_terms = jnp.zeros((1, HEAD_DIM), f32)
    scores = [
        dot(qg_ref[0, 0, :, cols], keys[:, cols], NT) * scale + bias_ref[...] for cols in heads
    ]
    prob_grads = [dot(qg_ref[0, 1, :, cols], values[:, cols], NT) for cols in heads]
    probs = []
    for h, cols in enumerate(heads):
        highest = jnp.max(scores[h], axis=-1, keepdims=True)
        terms = jnp.exp(scores[h] - highest)
        total = jnp.sum(terms, axis=-1, keepdims=True)
        probs.append(terms * (1.0 / total))
        columns = jnp.where(lane == 2 * h, highest + jnp.log(total), columns)
    outs = [dot(probs[h].astype(bf16), values[:, cols], NN).astype(bf16) for h, cols in enumerate(heads)]
    grads = []
    for h, cols in enumerate(heads):
        products = qg_ref[0, 1, :, cols].astype(f32) * outs[h].astype(f32)
        delta = jnp.sum(products, axis=-1, keepdims=True)
        columns = jnp.where(lane == 2 * h + 1, delta, columns)
        score_grad = (probs[h] * (prob_grads[h] - delta)).astype(bf16)
        grads.append(dot(score_grad, keys[:, cols], NN) * scale)
    for h, cols in enumerate(heads):
        qgrad_ref[:, cols], unit = norm_back(grads[h], q_ref[:, cols], qgain_ref[...])
        qn = qg_ref[0, 0, :, cols].astype(f32)
        q_terms += jnp.sum(grads[h] * unit, axis=0, keepdims=True)
        k_terms += jnp.sum(grads[h] * qn, axis=0, keepdims=True)
    sums_ref[0:1] = q_terms
    sums_ref[1:2] = k_terms / kgain_ref[...]
    stats_ref[...] = columns.T[:8]


def key_kernel(scale, n, bias_ref, *refs):
    stats, queries_in, keys_in = refs[:3], refs[3:6], refs[6 : 6 + n]
    outs, (queries, grads, keys, values) = refs[6 + n : -4], refs[-4:]
    _, _, tile, channels = queries_in[0].shape
    heads = head_cols(channels)
    fill(queries_in, queries, grads)
    fill(keys_in, keys, values)
    rows = jnp.concatenate([ref[...] for ref in stats], axis=1)
    scores = [dot(keys[:, cols], queries[:, cols], NT) * scale for cols in heads]
    prob_grads = [dot(values[:, cols], grads[:, cols], NT) for cols in heads]
    for h, cols in enumerate(heads):
        prob = jnp.exp(scores[h] + (bias_ref[...] - rows[2 * h : 2 * h + 1]))
        value_terms = dot(prob.astype(bf16), grads[:, cols], NN)
        score_grad = (prob * (prob_grads[h] - rows[2 * h + 1 : 2 * h + 2])).astype(bf16)
        key_terms = dot(score_grad, queries[:, cols], NN) * scale
        for i, ref in enumerate(outs):
            part = slice(i * tile, (i + 1) * tile)
            ref[0, 0, :, cols] = key_terms[part].astype(ref.dtype)
            ref[0, 1, :, cols] = value_terms[part].astype(ref.dtype)


def query_side(q, qg, qgain, kgain, bias, tiles, scale):
    _, _, tile, channels = qg.shape
    span = len(tiles) * tile
    qgrad = jax.ShapeDtypeStruct(q.shape, bf16)
    sums = jax.ShapeDtypeStruct((2, HEAD_DIM), f32)
    stats = jax.ShapeDtypeStruct((8, tile), f32)
    return pl.pallas_call(
        functools.partial(query_kernel, scale),
        out_shape=[qgrad, sums, stats],
        scratch_shapes=[
            pltpu.VMEM((span, channels), bf16),
            pltpu.VMEM((span, channels), bf16),
        ],
        compiler_params=pltpu.CompilerParams(vmem_limit_bytes=40 * 2**20),
        cost_estimate=COST,
        name="query_side",
    )(in_vmem(q), qg, qgain, kgain, bias, *map(in_vmem, tiles))


def key_side(bias, stats, queries, keys, types, scale):
    shape = keys[0].shape
    _, _, tile, channels = shape
    held = [pltpu.VMEM((n * tile, channels), bf16) for n in (3, 3, len(keys), len(keys))]
    return pl.pallas_call(
        functools.partial(key_kernel, scale, len(keys)),
        out_shape=[jax.ShapeDtypeStruct(shape, t) for t in types],
        scratch_shapes=held,
        compiler_params=pltpu.CompilerParams(vmem_limit_bytes=40 * 2**20),
        cost_estimate=COST,
        name="key_side",
    )(bias, *stats, *map(in_vmem, queries), *keys)


def finish_kernel(factor, k_ref, gain_ref, own_ref, mate_ref, sums_ref, *outs):
    kgrad_ref, vgrad_ref, *totals = outs
    for i, ref in enumerate(totals):
        ref[...] = sums_ref[i : i + 1] * factor
    part = kgrad_ref.shape[:-1] + (HEAD_DIM,)
    for cols in head_cols(k_ref.shape[-1]):
        total = [own_ref[0, i, :, cols] + mate_ref[0, i, :, cols].astype(f32) for i in range(2)]
        vgrad_ref[..., cols] = total[1].astype(bf16).reshape(part)
        kgrad, _ = norm_back(total[0], k_ref[:, cols], gain_ref[...])
        kgrad_ref[..., cols] = kgrad.reshape(part)


def finish(k, gain, own, mate, sums, shape, factor):
    total = jax.ShapeDtypeStruct((1, HEAD_DIM), f32)
    return pl.pallas_call(
        functools.partial(finish_kernel, factor),
        out_shape=[jax.ShapeDtypeStruct(shape, bf16)] * 2 + [total] * 2,
        cost_estimate=COST,
        name="finish",
    )(in_vmem(k), gain, in_vmem(own), in_vmem(mate), sums)


def in_vmem(x):
    return pltpu.with_memory_space_constraint(x, pltpu.VMEM)


def swapped(x, axis, bits):
    n = lax.axis_size(axis)
    return lax.ppermute(x, axis, [(i, i ^ bits) for i in range(n)])


def swap(x, axis):
    return swapped(x, axis, 1)


def rows_route(n, back=False):
    route = [(i, i + 2 - 4 * (i % 2)) for i in range(n)]
    return [(j, i) if back else (i, j) for i, j in route if 0 <= j < n]


def frames_route(n):
    return [(i, j) for i in range(n) for j in [i - 1 + 2 * (i % 2)] if 0 <= j < n]


def hop(x, back=False):
    return lax.ppermute(x, "height", rows_route(lax.axis_size("height"), back))


def far(x):
    return lax.ppermute(x, "tm", frames_route(lax.axis_size("tm")))


def level(total, axis, other, bits, other_bits):
    if axis == other:
        far = swapped(total, axis, bits ^ other_bits)
    else:
        n, m = lax.axis_size(axis), lax.axis_size(other)
        route = [
            (i * m + j, (i ^ bits) * m + (j ^ other_bits)) for i in range(n) for j in range(m)
        ]
        far = lax.ppermute(total, (axis, other), route)
    return (total + swapped(total, axis, bits)) + (swapped(total, other, other_bits) + far)


def together(steps, like, *args):
    always = lax.optimization_barrier(jnp.bool_(True))
    return lax.cond(always, steps, like, *args)


def frames(kv, qg):
    return swap(kv, "tm"), swap(qg, "tm"), far(kv), far(qg)


def last_levels(sums):
    n_tm, n_h = lax.axis_size("tm"), lax.axis_size("height")
    groups = [
        [t * n_h + r for t in range(a, n_tm, 2) for r in range(b, n_h, 2)]
        for a in range(2)
        for b in range(2)
    ]
    sent = jnp.broadcast_to(sums[None], (len(groups[0]),) + sums.shape)
    got = lax.all_to_all(sent, ("tm", "height"), 0, 0, axis_index_groups=groups)
    return jnp.sum(got, axis=0)


def after(x, first):
    return lax.optimization_barrier((x, first))[0]


def plus(a, b):
    return (a.astype(f32) + b.astype(f32)).astype(bf16)


def outside(axis):
    at, n = lax.axis_index(axis), lax.axis_size(axis)
    return (at == 0) | (at == n - 1)


def mask_bias(tile, rows):
    each = 3 if rows else 1
    slot = lax.broadcasted_iota(jnp.int32, (1, 3 * each * tile), 1) // tile
    gone = outside("tm") & (slot >= 2 * each)
    if rows:
        gone |= outside("height") & (slot % 3 == 2)
    return jnp.where(gone, MASKED, 0.0).astype(f32)


def with_sums(stats, sums):
    return stats.at[6:8, :HEAD_DIM].set(sums)


def shards(q_raw, k_raw, value_in, out_grad, q_gain, k_gain):
    shape = q_raw.shape
    channels = shape[-1]
    tile = math.prod(shape[:-1])
    scale = 1.0 / math.sqrt(HEAD_DIM)
    count = tile * (channels // HEAD_DIM)
    for axis in ("tm", "height", "heads"):
        count *= lax.axis_size(axis)
    qg_gain, kg_gain = q_gain.reshape(1, HEAD_DIM), k_gain.reshape(1, HEAD_DIM)

    (kv,) = norm_stack(k_raw, value_in, kg_gain)
    z = swap(kv, "height")
    qg, q_flat, k_flat = norm_stack(q_raw, out_grad, qg_gain, q_raw, k_raw)
    c0, d0, y0, w0 = together(frames, lambda a, b: (a, b, a, b), kv, qg)
    z, c0, d0, y0, w0 = lax.optimization_barrier((z, c0, d0, y0, w0))
    c1 = swap(z, "tm")
    x, y1 = hop(z), far(z)
    x, y1, c1 = lax.optimization_barrier((x, y1, c1))
    y2, c2 = far(x), swap(x, "tm")
    tiles = [kv, z, x, c0, c1, c2, y0, y1, y2]
    q_out, sums, stats = query_side(
        q_flat, qg, qg_gain, kg_gain, mask_bias(tile, True), tiles, scale
    )

    c_stats = swap(with_sums(stats, sums), "tm")
    sums = sums + c_stats[6:8, :HEAD_DIM]
    y_stats = far(stats)
    sums = level(sums, "heads", "heads", 1, 2)
    near = mask_bias(tile, False), [stats, c_stats, y_stats], [qg, d0, w0]
    (px,) = key_side(*near, [x], [bf16], scale)
    own, pz = key_side(*near, [kv, z], [f32, bf16], scale)
    px, sums = lax.optimization_barrier((px, sums))
    pz = plus(pz, hop(px, True))
    sums = sums + swap(sums, "height")
    pz, sums = lax.optimization_barrier((pz, sums))
    pz = swap(pz, "height")
    sums = together(last_levels, lambda t: t, sums)
    factor = 1.0 / math.sqrt(count)
    k_out, v_out, q_total, k_total = finish(k_flat, kg_gain, own, pz, sums, shape, factor)
    return q_out.reshape(shape), k_out, v_out, q_total.reshape(-1), k_total.reshape(-1)


def solution(mesh):
    split = P("tm", "height", None, "heads")
    return jax.shard_map(
        shards,
        mesh=mesh,
        in_specs=(split, split, split, split, P(), P()),
        out_specs=(split, split, split, P(), P()),
        check_vma=False,
    )
```

```python
import functools
import math

import jax
import jax.numpy as jnp
from jax import lax
from jax.experimental import pallas as pl
from jax.experimental.pallas import tpu as pltpu
from jax.sharding import PartitionSpec as P

HEAD_DIM = 128
EPS = 1e-06
MASKED = -1e30
NT = (((1,), (1,)), ((), ()))
NN = (((1,), (0,)), ((), ()))
TN = (((0,), (0,)), ((), ()))
f32 = jnp.float32
bf16 = jnp.bfloat16
COST = pl.CostEstimate(flops=10**6, bytes_accessed=10**5, transcendentals=0)


def dot(a, b, dims):
    return lax.dot_general(a, b, dims, preferred_element_type=f32)


def unit_of(raw):
    values = raw.astype(f32)
    inverse = lax.rsqrt(jnp.mean(values * values, axis=-1, keepdims=True) + EPS)
    return values * inverse, inverse


def head_cols(channels):
    return [slice(at, at + HEAD_DIM) for at in range(0, channels, HEAD_DIM)]


def stack_kernel(raw_ref, other_ref, gain_ref, *refs):
    flat_in, out_ref, flat_out = refs[: len(refs) // 2], refs[len(refs) // 2], refs[len(refs) // 2 + 1 :]
    tokens = out_ref.shape[2]
    for cols in head_cols(raw_ref.shape[-1]):
        unit, _ = unit_of(raw_ref[..., cols].reshape(tokens, HEAD_DIM))
        out_ref[0, 0, :, cols] = (unit * gain_ref[...]).astype(bf16)
        out_ref[0, 1, :, cols] = other_ref[..., cols].reshape(tokens, HEAD_DIM)
        for ref, flat_ref in zip(flat_in, flat_out):
            flat_ref[:, cols] = ref[..., cols].reshape(tokens, HEAD_DIM)


def norm_stack(raw, other, gain, *flat):
    tokens, channels = math.prod(raw.shape[:-1]), raw.shape[-1]
    return pl.pallas_call(
        stack_kernel,
        out_shape=[jax.ShapeDtypeStruct((1, 2, tokens, channels), bf16)]
        + [jax.ShapeDtypeStruct((tokens, channels), bf16) for _ in flat],
        cost_estimate=COST,
        name="norm_stack",
    )(raw, other, gain, *flat)


def fill(tiles, first, second):
    tile = tiles[0].shape[2]
    for i, ref in enumerate(tiles):
        rows = slice(i * tile, (i + 1) * tile)
        first[rows, :] = ref[0, 0]
        second[rows, :] = ref[0, 1]


def norm_back(grad_norm, raw, gain):
    unit, inverse = unit_of(raw)
    g = grad_norm * gain
    inner = jnp.mean(g * unit, axis=-1, keepdims=True)
    return ((g - unit * inner) * inverse).astype(bf16), unit


def near_kernel(scale, qg_ref, bias_ref, *refs):
    tiles, (terms_ref, prob_grads_ref, tops_ref, keys, values) = refs[:-5], refs[-5:]
    _, _, tile, channels = qg_ref.shape
    fill(tiles, keys, values)
    lane = lax.broadcasted_iota(jnp.int32, (tile, HEAD_DIM), 1)
    tops = jnp.zeros((tile, HEAD_DIM), f32)
    heads = head_cols(channels)
    scores = [
        dot(qg_ref[0, 0, :, cols], keys[:, cols], NT) * scale + bias_ref[...] for cols in heads
    ]
    for h, cols in enumerate(heads):
        prob_grads_ref[h] = dot(qg_ref[0, 1, :, cols], values[:, cols], NT)
        highest = jnp.max(scores[h], axis=-1, keepdims=True)
        terms = jnp.exp(scores[h] - highest)
        total = jnp.sum(terms, axis=-1, keepdims=True)
        terms_ref[h] = terms
        tops = jnp.where(lane == 2 * h, highest, jnp.where(lane == 2 * h + 1, total, tops))
    tops_ref[...] = tops


def query_kernel(scale, q_ref, qg_ref, qgain_ref, kgain_ref, bias_ref, *refs):
    tiles, (near_terms_ref, near_grads_ref, tops_ref, near_keys, near_values) = refs[:3], refs[3:8]
    qgrad_ref, sums_ref, stats_ref, keys, values = refs[8:]
    _, _, tile, channels = qg_ref.shape
    heads = head_cols(channels)
    fill(tiles, keys, values)
    lane = lax.broadcasted_iota(jnp.int32, (tile, HEAD_DIM), 1)
    columns = jnp.zeros((tile, HEAD_DIM), f32)
    q_terms = k_terms = jnp.zeros((1, HEAD_DIM), f32)
    scores = [
        dot(qg_ref[0, 0, :, cols], keys[:, cols], NT) * scale + bias_ref[...] for cols in heads
    ]
    prob_grads = [dot(qg_ref[0, 1, :, cols], values[:, cols], NT) for cols in heads]
    probs, near_probs = [], []
    for h in range(len(heads)):
        near_top = tops_ref[:, 2 * h : 2 * h + 1]
        highest = jnp.maximum(near_top, jnp.max(scores[h], axis=-1, keepdims=True))
        terms = jnp.exp(scores[h] - highest)
        near_scale = jnp.exp(near_top - highest)
        total = jnp.sum(terms, axis=-1, keepdims=True)
        total += tops_ref[:, 2 * h + 1 : 2 * h + 2] * near_scale
        inverse = 1.0 / total
        probs.append(terms * inverse)
        near_probs.append(near_terms_ref[h] * (near_scale * inverse))
        columns = jnp.where(lane == 2 * h, highest + jnp.log(total), columns)
    outs = []
    for h, cols in enumerate(heads):
        out = dot(near_probs[h].astype(bf16), near_values[:, cols], NN)
        outs.append((out + dot(probs[h].astype(bf16), values[:, cols], NN)).astype(bf16))
    grads = []
    for h, cols in enumerate(heads):
        products = qg_ref[0, 1, :, cols].astype(f32) * outs[h].astype(f32)
        delta = jnp.sum(products, axis=-1, keepdims=True)
        columns = jnp.where(lane == 2 * h + 1, delta, columns)
        score_grad = (probs[h] * (prob_grads[h] - delta)).astype(bf16)
        near_grad = (near_probs[h] * (near_grads_ref[h] - delta)).astype(bf16)
        grad = dot(near_grad, near_keys[:, cols], NN) + dot(score_grad, keys[:, cols], NN)
        grads.append(grad * scale)
    for h, cols in enumerate(heads):
        qgrad_ref[:, cols], unit = norm_back(grads[h], q_ref[:, cols], qgain_ref[...])
        qn = qg_ref[0, 0, :, cols].astype(f32)
        q_terms += jnp.sum(grads[h] * unit, axis=0, keepdims=True)
        k_terms += jnp.sum(grads[h] * qn, axis=0, keepdims=True)
    sums_ref[0:1] = q_terms
    sums_ref[1:2] = k_terms / kgain_ref[...]
    stats_ref[...] = columns.T[:8]


def pairs_kernel(scale, bias_ref, *refs):
    queries_in, keys_in, outs = refs[:3], refs[3:6], refs[6:12]
    queries, grads, keys, values = outs[4], outs[5], *refs[12:]
    tile = queries_in[0].shape[2]
    fill(queries_in, queries, grads)
    fill(keys_in, keys, values)
    near, far = slice(0, 2 * tile), slice(2 * tile, 3 * tile)
    for h, cols in enumerate(head_cols(queries.shape[1])):
        for rows, scores_ref, prob_grads_ref in ((near, *outs[:2]), (far, *outs[2:4])):
            scores = dot(keys[rows, cols], queries[:, cols], NT) * scale
            scores_ref[h] = scores + bias_ref[...]
            prob_grads_ref[h] = dot(values[rows, cols], grads[:, cols], NT)


def key_kernel(scale, scores_ref, prob_grads_ref, queries, grads, *refs):
    stats, outs = refs[:3], refs[3:]
    tile = outs[0].shape[2]
    rows = jnp.concatenate([ref[...] for ref in stats], axis=1)
    for h, cols in enumerate(head_cols(queries.shape[1])):
        prob = jnp.exp(scores_ref[h] - rows[2 * h : 2 * h + 1])
        value_terms = dot(prob.astype(bf16), grads[:, cols], NN)
        score_grad = (prob * (prob_grads_ref[h] - rows[2 * h + 1 : 2 * h + 2])).astype(bf16)
        key_terms = dot(score_grad, queries[:, cols], NN) * scale
        for i, ref in enumerate(outs):
            part = slice(i * tile, (i + 1) * tile)
            ref[0, 0, :, cols] = key_terms[part].astype(ref.dtype)
            ref[0, 1, :, cols] = value_terms[part].astype(ref.dtype)


def near_side(qg, bias, tiles, scale):
    _, _, tile, channels = qg.shape
    span, heads = len(tiles) * tile, channels // HEAD_DIM
    held = jax.ShapeDtypeStruct((span, channels), bf16)
    scores = jax.ShapeDtypeStruct((heads, tile, span), f32)
    return pl.pallas_call(
        functools.partial(near_kernel, scale),
        out_shape=[scores, scores, jax.ShapeDtypeStruct((tile, HEAD_DIM), f32), held, held],
        compiler_params=pltpu.CompilerParams(vmem_limit_bytes=40 * 2**20),
        cost_estimate=COST,
        name="near_side",
    )(qg, bias, *map(in_vmem, tiles))


def query_side(q, qg, qgain, kgain, bias, tiles, near, scale):
    _, _, tile, channels = qg.shape
    held = pltpu.VMEM((len(tiles) * tile, channels), bf16)
    return pl.pallas_call(
        functools.partial(query_kernel, scale),
        out_shape=[
            jax.ShapeDtypeStruct((tile, channels), bf16),
            jax.ShapeDtypeStruct((2, HEAD_DIM), f32),
            jax.ShapeDtypeStruct((8, tile), f32),
        ],
        scratch_shapes=[held, held],
        compiler_params=pltpu.CompilerParams(vmem_limit_bytes=40 * 2**20),
        cost_estimate=COST,
        name="query_side",
    )(in_vmem(q), qg, qgain, kgain, bias, *map(in_vmem, tiles), *map(in_vmem, near))


def pairs_side(bias, queries, keys, scale):
    _, _, tile, channels = keys[0].shape
    span, heads = 3 * tile, channels // HEAD_DIM
    shapes = [jax.ShapeDtypeStruct((heads, n * tile, span), f32) for n in (2, 2, 1, 1)]
    held = [jax.ShapeDtypeStruct((span, channels), bf16)] * 2
    return pl.pallas_call(
        functools.partial(pairs_kernel, scale),
        out_shape=shapes + held,
        scratch_shapes=[pltpu.VMEM((span, channels), bf16)] * 2,
        compiler_params=pltpu.CompilerParams(vmem_limit_bytes=40 * 2**20),
        cost_estimate=COST,
        name="pairs_side",
    )(bias, *map(in_vmem, queries), *map(in_vmem, keys))


def key_side(stats, scores, prob_grads, queries, grads, shape, types, scale):
    return pl.pallas_call(
        functools.partial(key_kernel, scale),
        out_shape=[jax.ShapeDtypeStruct(shape, t) for t in types],
        compiler_params=pltpu.CompilerParams(vmem_limit_bytes=40 * 2**20),
        cost_estimate=COST,
        name="key_side",
    )(*map(in_vmem, (scores, prob_grads, queries, grads)), *stats)


def finish_kernel(factor, k_ref, gain_ref, own_ref, mate_ref, sums_ref, *outs):
    kgrad_ref, vgrad_ref, *totals = outs
    for i, ref in enumerate(totals):
        ref[...] = sums_ref[i : i + 1] * factor
    part = kgrad_ref.shape[:-1] + (HEAD_DIM,)
    for cols in head_cols(k_ref.shape[-1]):
        total = [own_ref[0, i, :, cols] + mate_ref[0, i, :, cols].astype(f32) for i in range(2)]
        vgrad_ref[..., cols] = total[1].astype(bf16).reshape(part)
        kgrad, _ = norm_back(total[0], k_ref[:, cols], gain_ref[...])
        kgrad_ref[..., cols] = kgrad.reshape(part)


def finish(k, gain, own, mate, sums, shape, factor):
    total = jax.ShapeDtypeStruct((1, HEAD_DIM), f32)
    return pl.pallas_call(
        functools.partial(finish_kernel, factor),
        out_shape=[jax.ShapeDtypeStruct(shape, bf16)] * 2 + [total] * 2,
        cost_estimate=COST,
        name="finish",
    )(in_vmem(k), gain, in_vmem(own), in_vmem(mate), sums)


def in_vmem(x):
    return pltpu.with_memory_space_constraint(x, pltpu.VMEM)


def swapped(x, axis, bits):
    n = lax.axis_size(axis)
    return lax.ppermute(x, axis, [(i, i ^ bits) for i in range(n)])


def swap(x, axis):
    return swapped(x, axis, 1)


def rows_route(n, back=False):
    route = [(i, i + 2 - 4 * (i % 2)) for i in range(n)]
    return [(j, i) if back else (i, j) for i, j in route if 0 <= j < n]


def frames_route(n):
    return [(i, j) for i in range(n) for j in [i - 1 + 2 * (i % 2)] if 0 <= j < n]


def hop(x, back=False):
    return lax.ppermute(x, "height", rows_route(lax.axis_size("height"), back))


def far(x):
    return lax.ppermute(x, "tm", frames_route(lax.axis_size("tm")))


def level(total, axis, other, bits, other_bits):
    if axis == other:
        far = swapped(total, axis, bits ^ other_bits)
    else:
        n, m = lax.axis_size(axis), lax.axis_size(other)
        route = [
            (i * m + j, (i ^ bits) * m + (j ^ other_bits)) for i in range(n) for j in range(m)
        ]
        far = lax.ppermute(total, (axis, other), route)
    return (total + swapped(total, axis, bits)) + (swapped(total, other, other_bits) + far)


def together(steps, like, *args):
    always = lax.optimization_barrier(jnp.bool_(True))
    return lax.cond(always, steps, like, *args)


def frames(kv, qg):
    return swap(kv, "tm"), swap(qg, "tm"), far(kv), far(qg)


def last_levels(sums):
    n_tm, n_h = lax.axis_size("tm"), lax.axis_size("height")
    groups = [
        [t * n_h + r for t in range(a, n_tm, 2) for r in range(b, n_h, 2)]
        for a in range(2)
        for b in range(2)
    ]
    sent = jnp.broadcast_to(sums[None], (len(groups[0]),) + sums.shape)
    got = lax.all_to_all(sent, ("tm", "height"), 0, 0, axis_index_groups=groups)
    return jnp.sum(got, axis=0)


def after(x, first):
    return lax.optimization_barrier((x, first))[0]


def plus(a, b):
    return (a.astype(f32) + b.astype(f32)).astype(bf16)


def outside(axis):
    at, n = lax.axis_index(axis), lax.axis_size(axis)
    return (at == 0) | (at == n - 1)


def mask_bias(tile, tiles, far_from, beyond):
    slot = lax.broadcasted_iota(jnp.int32, (1, tiles * tile), 1) // tile
    gone = outside("tm") & (slot >= far_from)
    if beyond:
        gone |= outside("height")
    return jnp.where(gone, MASKED, 0.0).astype(f32)


def with_sums(stats, sums):
    return stats.at[6:8, :HEAD_DIM].set(sums)


def shards(q_raw, k_raw, value_in, out_grad, q_gain, k_gain):
    shape = q_raw.shape
    channels = shape[-1]
    tile = math.prod(shape[:-1])
    scale = 1.0 / math.sqrt(HEAD_DIM)
    count = tile * (channels // HEAD_DIM)
    for axis in ("tm", "height", "heads"):
        count *= lax.axis_size(axis)
    qg_gain, kg_gain = q_gain.reshape(1, HEAD_DIM), k_gain.reshape(1, HEAD_DIM)

    (kv,) = norm_stack(k_raw, value_in, kg_gain)
    z = swap(kv, "height")
    qg, q_flat, k_flat = norm_stack(q_raw, out_grad, qg_gain, q_raw, k_raw)
    c0, d0, y0, w0 = together(frames, lambda a, b: (a, b, a, b), kv, qg)
    z, c0, d0, y0, w0 = lax.optimization_barrier((z, c0, d0, y0, w0))
    c1 = swap(z, "tm")
    y1, x = far(z), hop(z)
    y1, c1, x = lax.optimization_barrier((y1, c1, x))
    y2, c2 = far(x), swap(x, "tm")
    near = near_side(qg, mask_bias(tile, 6, 4, False), [kv, z, c0, c1, y0, y1], scale)
    pairs = pairs_side(mask_bias(tile, 3, 2, False), [qg, d0, w0], [kv, z, x], scale)
    near, pairs = lax.optimization_barrier((near, pairs))
    far_bias = mask_bias(tile, 3, 2, True)
    q_out, sums, stats = query_side(
        q_flat, qg, qg_gain, kg_gain, far_bias, [x, c2, y2], near, scale
    )

    c_stats = swap(with_sums(stats, sums), "tm")
    sums = sums + c_stats[6:8, :HEAD_DIM]
    y_stats = far(stats)
    sums = level(sums, "heads", "heads", 1, 2)
    stats = [stats, c_stats, y_stats]
    near_pairs, far_pairs, held = pairs[:2], pairs[2:4], pairs[4:]
    (px,) = key_side(stats, *far_pairs, *held, kv.shape, [bf16], scale)
    own, pz = key_side(stats, *near_pairs, *held, kv.shape, [f32, bf16], scale)
    px, sums = lax.optimization_barrier((px, sums))
    pz = plus(pz, hop(px, True))
    sums = sums + swap(sums, "height")
    pz, sums = lax.optimization_barrier((pz, sums))
    pz = swap(pz, "height")
    sums = together(last_levels, lambda t: t, sums)
    factor = 1.0 / math.sqrt(count)
    k_out, v_out, q_total, k_total = finish(k_flat, kg_gain, own, pz, sums, shape, factor)
    return q_out.reshape(shape), k_out, v_out, q_total.reshape(-1), k_total.reshape(-1)


def solution(mesh):
    split = P("tm", "height", None, "heads")
    return jax.shard_map(
        shards,
        mesh=mesh,
        in_specs=(split, split, split, split, P(), P()),
        out_specs=(split, split, split, P(), P()),
        check_vma=False,
    )
```

```python
import functools
import math

import jax
import jax.numpy as jnp
from jax import lax
from jax.experimental import pallas as pl
from jax.experimental.pallas import tpu as pltpu
from jax.sharding import PartitionSpec as P

HEAD_DIM = 128
EPS = 1e-06
MASKED = -1e30
NT = (((1,), (1,)), ((), ()))
NN = (((1,), (0,)), ((), ()))
TN = (((0,), (0,)), ((), ()))
f32 = jnp.float32
bf16 = jnp.bfloat16
COST = pl.CostEstimate(flops=10**6, bytes_accessed=10**5, transcendentals=0)


def dot(a, b, dims):
    return lax.dot_general(a, b, dims, preferred_element_type=f32)


def unit_of(raw):
    values = raw.astype(f32)
    inverse = lax.rsqrt(jnp.mean(values * values, axis=-1, keepdims=True) + EPS)
    return values * inverse, inverse


def head_cols(channels):
    return [slice(at, at + HEAD_DIM) for at in range(0, channels, HEAD_DIM)]


def stack_kernel(raw_ref, other_ref, gain_ref, *refs):
    flat_in, out_ref, flat_out = refs[: len(refs) // 2], refs[len(refs) // 2], refs[len(refs) // 2 + 1 :]
    tokens = out_ref.shape[2]
    for cols in head_cols(raw_ref.shape[-1]):
        unit, _ = unit_of(raw_ref[..., cols].reshape(tokens, HEAD_DIM))
        out_ref[0, 0, :, cols] = (unit * gain_ref[...]).astype(bf16)
        out_ref[0, 1, :, cols] = other_ref[..., cols].reshape(tokens, HEAD_DIM)
        for ref, flat_ref in zip(flat_in, flat_out):
            flat_ref[:, cols] = ref[..., cols].reshape(tokens, HEAD_DIM)


def norm_stack(raw, other, gain, *flat):
    tokens, channels = math.prod(raw.shape[:-1]), raw.shape[-1]
    return pl.pallas_call(
        stack_kernel,
        out_shape=[jax.ShapeDtypeStruct((1, 2, tokens, channels), bf16)]
        + [jax.ShapeDtypeStruct((tokens, channels), bf16) for _ in flat],
        cost_estimate=COST,
        name="norm_stack",
    )(raw, other, gain, *flat)


def fill(tiles, first, second):
    tile = tiles[0].shape[2]
    for i, ref in enumerate(tiles):
        rows = slice(i * tile, (i + 1) * tile)
        first[rows, :] = ref[0, 0]
        second[rows, :] = ref[0, 1]


def norm_back(grad_norm, raw, gain):
    unit, inverse = unit_of(raw)
    g = grad_norm * gain
    inner = jnp.mean(g * unit, axis=-1, keepdims=True)
    return ((g - unit * inner) * inverse).astype(bf16), unit


def near_kernel(scale, qg_ref, bias_ref, *refs):
    tiles, (terms_ref, prob_grads_ref, tops_ref, keys, values) = refs[:-5], refs[-5:]
    _, _, tile, channels = qg_ref.shape
    fill(tiles, keys, values)
    lane = lax.broadcasted_iota(jnp.int32, (tile, HEAD_DIM), 1)
    tops = jnp.zeros((tile, HEAD_DIM), f32)
    heads = head_cols(channels)
    scores = [
        dot(qg_ref[0, 0, :, cols], keys[:, cols], NT) * scale + bias_ref[...] for cols in heads
    ]
    for h, cols in enumerate(heads):
        prob_grads_ref[h] = dot(qg_ref[0, 1, :, cols], values[:, cols], NT)
        highest = jnp.max(scores[h], axis=-1, keepdims=True)
        terms = jnp.exp(scores[h] - highest)
        total = jnp.sum(terms, axis=-1, keepdims=True)
        terms_ref[h] = terms
        tops = jnp.where(lane == 2 * h, highest, jnp.where(lane == 2 * h + 1, total, tops))
    tops_ref[...] = tops


def query_kernel(scale, q_ref, qg_ref, qgain_ref, kgain_ref, bias_ref, *refs):
    tiles, (near_terms_ref, near_grads_ref, tops_ref, near_keys, near_values) = refs[:3], refs[3:8]
    qgrad_ref, sums_ref, stats_ref, keys, values = refs[8:]
    _, _, tile, channels = qg_ref.shape
    heads = head_cols(channels)
    fill(tiles, keys, values)
    lane = lax.broadcasted_iota(jnp.int32, (tile, HEAD_DIM), 1)
    columns = jnp.zeros((tile, HEAD_DIM), f32)
    q_terms = k_terms = jnp.zeros((1, HEAD_DIM), f32)
    scores = [
        dot(qg_ref[0, 0, :, cols], keys[:, cols], NT) * scale + bias_ref[...] for cols in heads
    ]
    prob_grads = [dot(qg_ref[0, 1, :, cols], values[:, cols], NT) for cols in heads]
    probs, near_probs = [], []
    for h in range(len(heads)):
        near_top = tops_ref[:, 2 * h : 2 * h + 1]
        highest = jnp.maximum(near_top, jnp.max(scores[h], axis=-1, keepdims=True))
        terms = jnp.exp(scores[h] - highest)
        near_scale = jnp.exp(near_top - highest)
        total = jnp.sum(terms, axis=-1, keepdims=True)
        total += tops_ref[:, 2 * h + 1 : 2 * h + 2] * near_scale
        inverse = 1.0 / total
        probs.append(terms * inverse)
        near_probs.append(near_terms_ref[h] * (near_scale * inverse))
        columns = jnp.where(lane == 2 * h, highest + jnp.log(total), columns)
    outs = []
    for h, cols in enumerate(heads):
        out = dot(near_probs[h].astype(bf16), near_values[:, cols], NN)
        outs.append((out + dot(probs[h].astype(bf16), values[:, cols], NN)).astype(bf16))
    grads = []
    for h, cols in enumerate(heads):
        products = qg_ref[0, 1, :, cols].astype(f32) * outs[h].astype(f32)
        delta = jnp.sum(products, axis=-1, keepdims=True)
        columns = jnp.where(lane == 2 * h + 1, delta, columns)
        score_grad = (probs[h] * (prob_grads[h] - delta)).astype(bf16)
        near_grad = (near_probs[h] * (near_grads_ref[h] - delta)).astype(bf16)
        grad = dot(near_grad, near_keys[:, cols], NN) + dot(score_grad, keys[:, cols], NN)
        grads.append(grad * scale)
    for h, cols in enumerate(heads):
        qgrad_ref[:, cols], unit = norm_back(grads[h], q_ref[:, cols], qgain_ref[...])
        qn = qg_ref[0, 0, :, cols].astype(f32)
        q_terms += jnp.sum(grads[h] * unit, axis=0, keepdims=True)
        k_terms += jnp.sum(grads[h] * qn, axis=0, keepdims=True)
    sums_ref[0:1] = q_terms
    sums_ref[1:2] = k_terms / kgain_ref[...]
    stats_ref[...] = columns.T[:8]


def pairs_kernel(scale, bias_ref, *refs):
    queries_in, keys_in, outs = refs[:3], refs[3:6], refs[6:12]
    queries, grads, keys, values = outs[4], outs[5], *refs[12:]
    tile = queries_in[0].shape[2]
    fill(queries_in, queries, grads)
    fill(keys_in, keys, values)
    near, far = slice(0, 2 * tile), slice(2 * tile, 3 * tile)
    for h, cols in enumerate(head_cols(queries.shape[1])):
        for rows, scores_ref, prob_grads_ref in ((near, *outs[:2]), (far, *outs[2:4])):
            scores = dot(keys[rows, cols], queries[:, cols], NT) * scale
            scores_ref[h] = scores + bias_ref[...]
            prob_grads_ref[h] = dot(values[rows, cols], grads[:, cols], NT)


def key_kernel(scale, scores_ref, prob_grads_ref, queries, grads, *refs):
    stats, outs = refs[:3], refs[3:]
    tile = outs[0].shape[2]
    rows = jnp.concatenate([ref[...] for ref in stats], axis=1)
    for h, cols in enumerate(head_cols(queries.shape[1])):
        prob = jnp.exp(scores_ref[h] - rows[2 * h : 2 * h + 1])
        value_terms = dot(prob.astype(bf16), grads[:, cols], NN)
        score_grad = (prob * (prob_grads_ref[h] - rows[2 * h + 1 : 2 * h + 2])).astype(bf16)
        key_terms = dot(score_grad, queries[:, cols], NN) * scale
        for i, ref in enumerate(outs):
            part = slice(i * tile, (i + 1) * tile)
            ref[0, 0, :, cols] = key_terms[part].astype(ref.dtype)
            ref[0, 1, :, cols] = value_terms[part].astype(ref.dtype)


def early_kernel(scale, qg_ref, near_bias_ref, bias_ref, *refs):
    near_in, pairs_in, near_outs, pairs_refs = refs[:6], refs[6:12], refs[12:17], refs[17:]
    near_kernel(scale, qg_ref, near_bias_ref, *near_in, *near_outs)
    pairs_kernel(scale, bias_ref, *pairs_in, *pairs_refs)


def early_side(qg, near_bias, bias, tiles, queries, keys, scale):
    _, _, tile, channels = qg.shape
    span, heads = len(tiles) * tile, channels // HEAD_DIM
    held = jax.ShapeDtypeStruct((span, channels), bf16)
    scores = jax.ShapeDtypeStruct((heads, tile, span), f32)
    near = [scores, scores, jax.ShapeDtypeStruct((tile, HEAD_DIM), f32), held, held]
    row = len(queries) * tile
    pairs = [jax.ShapeDtypeStruct((heads, n * tile, row), f32) for n in (2, 2, 1, 1)]
    pairs += [jax.ShapeDtypeStruct((row, channels), bf16)] * 2
    outs = pl.pallas_call(
        functools.partial(early_kernel, scale),
        out_shape=near + pairs,
        scratch_shapes=[pltpu.VMEM((row, channels), bf16)] * 2,
        compiler_params=pltpu.CompilerParams(vmem_limit_bytes=48 * 2**20),
        cost_estimate=COST,
        name="early_side",
    )(qg, near_bias, bias, *map(in_vmem, [*tiles, *queries, *keys]))
    return outs[:5], outs[5:]


def query_side(q, qg, qgain, kgain, bias, tiles, near, scale):
    _, _, tile, channels = qg.shape
    held = pltpu.VMEM((len(tiles) * tile, channels), bf16)
    return pl.pallas_call(
        functools.partial(query_kernel, scale),
        out_shape=[
            jax.ShapeDtypeStruct((tile, channels), bf16),
            jax.ShapeDtypeStruct((2, HEAD_DIM), f32),
            jax.ShapeDtypeStruct((8, tile), f32),
        ],
        scratch_shapes=[held, held],
        compiler_params=pltpu.CompilerParams(vmem_limit_bytes=40 * 2**20),
        cost_estimate=COST,
        name="query_side",
    )(in_vmem(q), qg, qgain, kgain, bias, *map(in_vmem, tiles), *map(in_vmem, near))


def key_side(stats, scores, prob_grads, queries, grads, shape, types, scale):
    return pl.pallas_call(
        functools.partial(key_kernel, scale),
        out_shape=[jax.ShapeDtypeStruct(shape, t) for t in types],
        compiler_params=pltpu.CompilerParams(vmem_limit_bytes=40 * 2**20),
        cost_estimate=COST,
        name="key_side",
    )(*map(in_vmem, (scores, prob_grads, queries, grads)), *stats)


def finish_kernel(factor, k_ref, gain_ref, own_ref, mate_ref, sums_ref, *outs):
    kgrad_ref, vgrad_ref, *totals = outs
    for i, ref in enumerate(totals):
        ref[...] = sums_ref[i : i + 1] * factor
    part = kgrad_ref.shape[:-1] + (HEAD_DIM,)
    for cols in head_cols(k_ref.shape[-1]):
        total = [own_ref[0, i, :, cols] + mate_ref[0, i, :, cols].astype(f32) for i in range(2)]
        vgrad_ref[..., cols] = total[1].astype(bf16).reshape(part)
        kgrad, _ = norm_back(total[0], k_ref[:, cols], gain_ref[...])
        kgrad_ref[..., cols] = kgrad.reshape(part)


def finish(k, gain, own, mate, sums, shape, factor):
    total = jax.ShapeDtypeStruct((1, HEAD_DIM), f32)
    return pl.pallas_call(
        functools.partial(finish_kernel, factor),
        out_shape=[jax.ShapeDtypeStruct(shape, bf16)] * 2 + [total] * 2,
        cost_estimate=COST,
        name="finish",
    )(in_vmem(k), gain, in_vmem(own), in_vmem(mate), sums)


def in_vmem(x):
    return pltpu.with_memory_space_constraint(x, pltpu.VMEM)


def swapped(x, axis, bits):
    n = lax.axis_size(axis)
    return lax.ppermute(x, axis, [(i, i ^ bits) for i in range(n)])


def swap(x, axis):
    return swapped(x, axis, 1)


def rows_route(n, back=False):
    route = [(i, i + 2 - 4 * (i % 2)) for i in range(n)]
    return [(j, i) if back else (i, j) for i, j in route if 0 <= j < n]


def frames_route(n):
    return [(i, j) for i in range(n) for j in [i - 1 + 2 * (i % 2)] if 0 <= j < n]


def hop(x, back=False):
    return lax.ppermute(x, "height", rows_route(lax.axis_size("height"), back))


def far(x):
    return lax.ppermute(x, "tm", frames_route(lax.axis_size("tm")))


def level(total, axis, other, bits, other_bits):
    if axis == other:
        far = swapped(total, axis, bits ^ other_bits)
    else:
        n, m = lax.axis_size(axis), lax.axis_size(other)
        route = [
            (i * m + j, (i ^ bits) * m + (j ^ other_bits)) for i in range(n) for j in range(m)
        ]
        far = lax.ppermute(total, (axis, other), route)
    return (total + swapped(total, axis, bits)) + (swapped(total, other, other_bits) + far)


def together(steps, like, *args):
    always = lax.optimization_barrier(jnp.bool_(True))
    return lax.cond(always, steps, like, *args)


def frames(kv, qg):
    return swap(kv, "tm"), swap(qg, "tm"), far(kv), far(qg)


def last_levels(sums):
    n_tm, n_h = lax.axis_size("tm"), lax.axis_size("height")
    groups = [
        [t * n_h + r for t in range(a, n_tm, 2) for r in range(b, n_h, 2)]
        for a in range(2)
        for b in range(2)
    ]
    sent = jnp.broadcast_to(sums[None], (len(groups[0]),) + sums.shape)
    got = lax.all_to_all(sent, ("tm", "height"), 0, 0, axis_index_groups=groups)
    return jnp.sum(got, axis=0)


def after(x, first):
    return lax.optimization_barrier((x, first))[0]


def plus(a, b):
    return (a.astype(f32) + b.astype(f32)).astype(bf16)


def outside(axis):
    at, n = lax.axis_index(axis), lax.axis_size(axis)
    return (at == 0) | (at == n - 1)


def mask_bias(tile, tiles, far_from, beyond):
    slot = lax.broadcasted_iota(jnp.int32, (1, tiles * tile), 1) // tile
    gone = outside("tm") & (slot >= far_from)
    if beyond:
        gone |= outside("height")
    return jnp.where(gone, MASKED, 0.0).astype(f32)


def with_sums(stats, sums):
    return stats.at[6:8, :HEAD_DIM].set(sums)


def shards(q_raw, k_raw, value_in, out_grad, q_gain, k_gain):
    shape = q_raw.shape
    channels = shape[-1]
    tile = math.prod(shape[:-1])
    scale = 1.0 / math.sqrt(HEAD_DIM)
    count = tile * (channels // HEAD_DIM)
    for axis in ("tm", "height", "heads"):
        count *= lax.axis_size(axis)
    qg_gain, kg_gain = q_gain.reshape(1, HEAD_DIM), k_gain.reshape(1, HEAD_DIM)

    (kv,) = norm_stack(k_raw, value_in, kg_gain)
    z = swap(kv, "height")
    qg, q_flat, k_flat = norm_stack(q_raw, out_grad, qg_gain, q_raw, k_raw)
    c0, d0, y0, w0 = together(frames, lambda a, b: (a, b, a, b), kv, qg)
    z, c0, d0, y0, w0 = lax.optimization_barrier((z, c0, d0, y0, w0))
    c1 = swap(z, "tm")
    y1, x = far(z), hop(z)
    y1, c1, x = lax.optimization_barrier((y1, c1, x))
    y2, c2 = far(x), swap(x, "tm")
    near, pairs = early_side(
        qg,
        mask_bias(tile, 6, 4, False),
        mask_bias(tile, 3, 2, False),
        [kv, z, c0, c1, y0, y1],
        [qg, d0, w0],
        [kv, z, x],
        scale,
    )
    near, pairs = lax.optimization_barrier((near, pairs))
    far_bias = mask_bias(tile, 3, 2, True)
    q_out, sums, stats = query_side(
        q_flat, qg, qg_gain, kg_gain, far_bias, [x, c2, y2], near, scale
    )

    c_stats = swap(with_sums(stats, sums), "tm")
    sums = sums + c_stats[6:8, :HEAD_DIM]
    y_stats = far(stats)
    sums = level(sums, "heads", "heads", 1, 2)
    stats = [stats, c_stats, y_stats]
    near_pairs, far_pairs, held = pairs[:2], pairs[2:4], pairs[4:]
    (px,) = key_side(stats, *far_pairs, *held, kv.shape, [bf16], scale)
    own, pz = key_side(stats, *near_pairs, *held, kv.shape, [f32, bf16], scale)
    px, sums = lax.optimization_barrier((px, sums))
    pz = plus(pz, hop(px, True))
    sums = sums + swap(sums, "height")
    pz, sums = lax.optimization_barrier((pz, sums))
    pz = swap(pz, "height")
    sums = together(last_levels, lambda t: t, sums)
    factor = 1.0 / math.sqrt(count)
    k_out, v_out, q_total, k_total = finish(k_flat, kg_gain, own, pz, sums, shape, factor)
    return q_out.reshape(shape), k_out, v_out, q_total.reshape(-1), k_total.reshape(-1)


def solution(mesh):
    split = P("tm", "height", None, "heads")
    return jax.shard_map(
        shards,
        mesh=mesh,
        in_specs=(split, split, split, split, P(), P()),
        out_specs=(split, split, split, P(), P()),
        check_vma=False,
    )
```
